32 devices in a mesh: dp: 4 (over y, x), seq: 4 (over z), fsdp: 2 (over core).
Axes of the slice: x: 2, y: 2, z: 4, core: 2. Of those that a mesh axis runs over, the one named last changes fastest.
Arguments:
- inputs: bfloat16 [8, 1024, 2048], P('dp', ('seq', 'fsdp')), may hold values from -6 to 6
- block_ids: int32 [8, 1024], P('dp', ('seq', 'fsdp')), may hold values from 0 to 7, never falling along the last dimension, each value on 1 to 256 neighbouring positions
- gain_one: bfloat16 [2048], P(('dp', 'seq', 'fsdp')), may hold values from 0.5 to 1.5
- beta_one: bfloat16 [2048], P(('dp', 'seq', 'fsdp')), may hold values from -3 to 3
- w_qkv: bfloat16 [2048, 6144], P(('dp', 'seq', 'fsdp')), may hold values from -0.125 to 0.125
- bias_query: bfloat16 [2048], P(('dp', 'seq', 'fsdp')), may hold values from -3 to 3
- bias_value: bfloat16 [2048], P(('dp', 'seq', 'fsdp')), may hold values from -3 to 3
- w_out: bfloat16 [2048, 2048], P(('dp', 'seq', 'fsdp')), may hold values from -0.375 to 0.375
- bias_out: bfloat16 [2048], P(('dp', 'seq', 'fsdp')), may hold values from -3 to 3
- gain_two: bfloat16 [2048], P(('dp', 'seq', 'fsdp')), may hold values from 0.5 to 1.5
- beta_two: bfloat16 [2048], P(('dp', 'seq', 'fsdp')), may hold values from -3 to 3
- w_up: bfloat16 [2048, 8192], P(('dp', 'seq', 'fsdp')), may hold values from -0.125 to 0.125
- bias_up: bfloat16 [8192], P(('dp', 'seq', 'fsdp')), may hold values from -3 to 3
- w_down: bfloat16 [8192, 2048], P(('dp', 'seq', 'fsdp')), may hold values from -0.09375 to 0.09375
- bias_down: bfloat16 [2048], P(('dp', 'seq', 'fsdp')), may hold values from -3 to 3
- cotangent: bfloat16 [8, 1024, 2048], P('dp', ('seq', 'fsdp')), may hold values from -6 to 6
Outputs:
- outputs: bfloat16 [8, 1024, 2048], P('dp', ('seq', 'fsdp'))
- grad_inputs: float32 [8, 1024, 2048], P('dp', ('seq', 'fsdp'))
- grad_w_qkv: float32 [2048, 6144], P(('dp', 'seq', 'fsdp'))
- grad_bias_query: float32 [2048], P(('dp', 'seq', 'fsdp'))
- grad_bias_value: float32 [2048], P(('dp', 'seq', 'fsdp'))
- grad_w_out: float32 [2048, 2048], P(('dp', 'seq', 'fsdp'))
- grad_bias_out: float32 [2048], P(('dp', 'seq', 'fsdp'))
- grad_gain_one: float32 [2048], P(('dp', 'seq', 'fsdp'))
- grad_beta_one: float32 [2048], P(('dp', 'seq', 'fsdp'))
- grad_w_up: float32 [2048, 8192], P(('dp', 'seq', 'fsdp'))
- grad_bias_up: float32 [8192], P(('dp', 'seq', 'fsdp'))
- grad_w_down: float32 [8192, 2048], P(('dp', 'seq', 'fsdp'))
- grad_bias_down: float32 [2048], P(('dp', 'seq', 'fsdp'))
- grad_gain_two: float32 [2048], P(('dp', 'seq', 'fsdp'))
- grad_beta_two: float32 [2048], P(('dp', 'seq', 'fsdp'))
The draws below stay inside these ranges and needn't reach their ends.
Inputs may be any that keep to these rules, and one draw needn't show every extreme that they name: `block_ids`: within each sequence the block ids start at 0 and never fall, rising by at most one from token to token; each block holds 1 to 256 tokens and one block of each sequence holds exactly 256.
All inputs are finite; a program needn't handle non-finite values.
Results may differ from the reference program's by a relative error of at most 0.013.
Values may be sent and summed in bfloat16 or wider, within the bound.
No kernel may reach another device: no remote copies, remote signals or barrier semaphores. Data moves between devices by JAX's collectives and lax.ppermute only.
A program may use at most 512 MiB of HBM per device.

```python
import math
import jax
import jax.numpy as jnp
import numpy as np
from jax import lax

HEADS = 16
HEAD_DIM = 128
FF = 8192
BLOCK = 256
D = 2048
LENGTH = 1024
SEQS = 8


def level_of(rng, dims, cuts, low, high):
    def one(axis_at, parts):
        heights = jax.random.uniform(jax.random.fold_in(jax.random.fold_in(rng, 6), axis_at), (parts,), jnp.float32, low / len(cuts), high / len(cuts))
        return jnp.repeat(jnp.exp(heights), dims[axis_at] // parts).reshape((-1,) + (1,) * (len(dims) - axis_at - 1))

    loudness = one(*cuts[0])
    for cut in cuts[1:]:
        loudness = loudness * one(*cut)
    return loudness


def profile(number_of, total, most, skew):
    weights = [(1 << 20) // math.isqrt(rank ** skew) + 1 for rank in range(2, number_of + 1)]
    rest, counts = total - most - (number_of - 1), [1] * (number_of - 1)
    while rest > 0:
        free = [i for i in range(number_of - 1) if counts[i] < most]
        pool, remaining = sum([weights[i] for i in free]), rest
        for i in free:
            more = min(most - counts[i], max(1, remaining * weights[i] // pool), rest)
            counts[i] = counts[i] + more
            rest = rest - more
    return np.array([most] + counts)


def ragged(rng, amount, total, reach, slope):
    if amount == 2:
        one = jax.random.randint(rng, (), max(1, total - reach), min(reach, total - 1) + 1)
        return jnp.stack([one, total - one])
    tallies = jnp.asarray(profile(amount, total, reach, slope), jnp.int32)
    twos = (amount - 1) // 2
    donor, receiver = tallies[1:1 + 2 * twos:2], tallies[2:2 + 2 * twos:2]
    margin = jnp.minimum(donor - 1, reach - receiver)
    shifted = jax.random.randint(jax.random.fold_in(rng, 1), (twos,), 0, 1 << 20) % (margin + 1)
    tallies = tallies.at[1:1 + 2 * twos:2].set(donor - shifted).at[2:2 + 2 * twos:2].set(receiver + shifted)
    return tallies[jax.random.permutation(jax.random.fold_in(rng, 2), amount)]


def centred(rng, extent, width, limit, shards=(), kind=jnp.bfloat16):
    values = jax.random.normal(rng, extent, jnp.float32) * width
    if len(shards) > 0:
        values = level_of(rng, extent, shards, -0.22, 0.18) * values
    return jnp.clip(values, min=-limit, max=limit).astype(kind)


def setup_inputs(seed: int = 0) -> dict:
    keys = jax.random.split(jax.random.key(seed), 17)
    return {
        "inputs": centred(keys[0], (SEQS, LENGTH, D), 1.0, 6.0, ((0, 4), (1, 8))),
        "block_ids": jax.vmap(lambda own: jnp.searchsorted(jnp.cumsum(ragged(own, 2 * LENGTH // BLOCK, LENGTH, BLOCK, 2)), jnp.arange(LENGTH), side="right"))(jax.random.split(keys[1], SEQS)).reshape((SEQS, LENGTH)).astype(jnp.int32),
        "gain_one": jnp.clip(1.0 + 0.1 * jax.random.normal(keys[2], (D,), jnp.float32), 0.5, 1.5).astype(jnp.bfloat16),
        "beta_one": centred(keys[3], (D,), 0.5, 3.0, ((0, 32),)),
        "w_qkv": centred(keys[4], (D, 3 * D), D ** -0.5, 0.125, ((0, 32),)),
        "bias_query": centred(keys[5], (D,), 0.5, 3.0, ((0, 32),)),
        "bias_value": centred(keys[6], (D,), 0.5, 3.0, ((0, 32),)),
        "w_out": centred(keys[7], (D, D), (D // 8) ** -0.5, 0.375, ((0, 32),)),
        "bias_out": centred(keys[8], (D,), 0.5, 3.0, ((0, 32),)),
        "gain_two": jnp.clip(1.0 + 0.1 * jax.random.normal(keys[9], (D,), jnp.float32), 0.5, 1.5).astype(jnp.bfloat16),
        "beta_two": centred(keys[10], (D,), 0.5, 3.0, ((0, 32),)),
        "w_up": centred(keys[11], (D, FF), D ** -0.5, 0.125, ((0, 32),)),
        "bias_up": centred(keys[12], (FF,), 0.5, 3.0, ((0, 32),)),
        "w_down": centred(keys[13], (FF, D), (FF // 2) ** -0.5, 0.09375, ((0, 32),)),
        "bias_down": centred(keys[14], (D,), 0.5, 3.0, ((0, 32),)),
        "cotangent": centred(keys[15], (SEQS, LENGTH, D), 1.0, 6.0, ((0, 4), (1, 8))),
    }


@jax.custom_vjp
def low(v):
    return lax.optimization_barrier(v.astype(jnp.bfloat16)).astype(jnp.float32)

@jax.custom_vjp
def low_back(v):
    return v

def low_keep(v):
    return (low(v), None)

def low_pass(kept, grad):
    return (grad,)

def back_keep(v):
    return (v, None)

def back_low(kept, grad):
    return (low(grad),)
low.defvjp(low_keep, low_pass)
low_back.defvjp(back_keep, back_low)
EPSILON = 1e-05

def layer_norm(values, gain, shift):
    average = lax.optimization_barrier(jnp.mean(values, axis=-1, keepdims=True))
    centered = values - average
    variance = lax.optimization_barrier(jnp.mean(centered * centered, axis=-1, keepdims=True))
    return centered * lax.rsqrt(variance + EPSILON) * gain + shift

def matmul(left, right):
    return jnp.dot(left, right, precision=lax.Precision.HIGHEST, preferred_element_type=jnp.float32)

def reference(inputs, block_ids, gain_one, beta_one, w_qkv, bias_query, bias_value, w_out, bias_out, gain_two, beta_two, w_up, bias_up, w_down, bias_down, cotangent):
    score_scale = HEAD_DIM ** (-0.5)
    positions = jnp.arange(LENGTH, dtype=jnp.float32)
    distance = jnp.abs(positions[:, None] - positions[None, :])
    slopes = jnp.exp2(-8.0 * (jnp.arange(HEADS, dtype=jnp.float32) + 1.0) / HEADS)

    def forward(tokens, g_one, b_one, qkv_weight, q_bias, v_bias, out_weight, out_bias, g_two, b_two, up_weight, up_bias, down_weight, down_bias):

        def one_sequence(item):
            seq_tokens, seq_ids = item
            normed_one = low(layer_norm(seq_tokens, g_one, b_one))
            projected = matmul(normed_one, qkv_weight)
            query = low(low_back(projected[:, :D] + q_bias))
            keys_proj = low(low_back(projected[:, D:2 * D]))
            value = low(low_back(projected[:, 2 * D:] + v_bias))
            query_heads = query.reshape(LENGTH, HEADS, HEAD_DIM)
            key_heads = keys_proj.reshape(LENGTH, HEADS, HEAD_DIM)
            value_heads = value.reshape(LENGTH, HEADS, HEAD_DIM)
            raw_scores = low_back(jnp.einsum('qhd,khd->hqk', query_heads, key_heads, precision=lax.Precision.HIGHEST))
            scores = raw_scores * score_scale - slopes[:, None, None] * distance
            allowed = seq_ids[None, :] <= seq_ids[:, None]
            scores = jnp.where(allowed[None], scores, -1e+30)
            row_max = lax.optimization_barrier(jnp.max(scores, axis=-1, keepdims=True))
            exponent = jnp.exp(scores - row_max)
            probs = exponent / lax.optimization_barrier(jnp.sum(exponent, axis=-1, keepdims=True))
            attention = jnp.einsum('hqk,khd->qhd', low(probs), value_heads, precision=lax.Precision.HIGHEST).reshape(LENGTH, D)
            context = low(low_back(attention))
            residual = seq_tokens + low_back(matmul(context, out_weight)) + out_bias
            normed_two = low(layer_norm(residual, g_two, b_two))
            hidden = low_back(matmul(normed_two, up_weight) + up_bias)
            activated = low(jax.nn.gelu(hidden, approximate=True))
            return residual + matmul(activated, down_weight) + down_bias
        return lax.map(jax.checkpoint(one_sequence), (tokens, block_ids))
    floats = [arg.astype(jnp.float32) for arg in (inputs, gain_one, beta_one, w_qkv, bias_query, bias_value, w_out, bias_out, gain_two, beta_two, w_up, bias_up, w_down, bias_down)]
    result, backward = jax.vjp(forward, *floats)
    grads = backward(cotangent.astype(jnp.float32))
    return (result.astype(jnp.bfloat16), grads[0], grads[3], grads[4], grads[5], grads[6], grads[7], grads[1], grads[2], grads[10], grads[11], grads[12], grads[13], grads[8], grads[9])
```

```python
import jax
import jax.numpy as jnp
from jax import lax
from jax.experimental import pallas as pl
from jax.experimental.pallas import tpu as pltpu
from jax.sharding import PartitionSpec as P

HEAD_DIM = 128
EPSILON = 1e-05
ALL = ("dp", "seq", "fsdp")
LINE = ("seq", "fsdp")
f32 = jnp.float32
bf16 = jnp.bfloat16


def dot(left, right, dims):
    return lax.dot_general(left, right, (dims, ((), ())), preferred_element_type=f32)


def norm_parts(values):
    average = jnp.mean(values, axis=-1, keepdims=True)
    centered = values - average
    variance = jnp.mean(centered * centered, axis=-1, keepdims=True)
    scale = lax.rsqrt(variance + EPSILON)
    return centered * scale, scale


def norm_back(grad, gain, normal, scale):
    scaled = grad * gain
    return scale * (
        scaled
        - jnp.mean(scaled, axis=-1, keepdims=True)
        - normal * jnp.mean(scaled * normal, axis=-1, keepdims=True)
    )


def gelu_both(hidden):
    root = (2.0 / jnp.pi) ** 0.5
    square = hidden * hidden
    tanh = jnp.tanh(root * (hidden + 0.044715 * hidden * square))
    half = 0.5 * (1.0 + tanh)
    slope = half + 0.5 * hidden * (1.0 - tanh * tanh) * root * (1.0 + 3 * 0.044715 * square)
    return hidden * half, slope


def permute(value, axis, mask):
    count = lax.axis_size(axis)
    return lax.ppermute(value, axis, [(i, i ^ mask) for i in range(count)])


def gather_dp(block):
    if lax.axis_size("dp") != 4:
        return lax.all_gather(block, "dp", axis=0, tiled=False)
    half = block.shape[0] // 2
    one = permute(block, "dp", 1)
    two = permute(block, "dp", 2)
    top = permute(two[:half], "dp", 1)
    low = permute(one[half:], "dp", 2)
    return jnp.stack([block, one, two, jnp.concatenate([top, low], axis=0)])


def gather_dp_rows(block):
    return lax.all_gather(block, "dp", axis=0, tiled=True)


def scatter_dp(parts):
    if lax.axis_size("dp") != 4:
        return lax.psum_scatter(parts.astype(bf16), "dp", scatter_dimension=0, tiled=False).astype(f32)
    half = parts.shape[1] // 2
    low = parts[3].astype(bf16)
    from_one = permute(low[:half], "dp", 1).astype(f32)
    from_two = permute(low[half:], "dp", 2).astype(f32)
    two = jnp.concatenate([parts[2, :half] + from_one, parts[2, half:]], axis=0)
    one = jnp.concatenate([parts[1, :half], parts[1, half:] + from_two], axis=0)
    return (
        parts[0]
        + permute(one.astype(bf16), "dp", 1).astype(f32)
        + permute(two.astype(bf16), "dp", 2).astype(f32)
    )


BLOCK = 256
LOG2E = 1.4426950408889634
VMEM_BYTES = 56 * 2**20


def call(body, **options):
    return pl.pallas_call(
        body, compiler_params=pltpu.CompilerParams(vmem_limit_bytes=VMEM_BYTES), **options
    )


def norm_project_body(x_ref, gain_ref, beta_ref, w_ref, bias_ref, normed_ref, out_ref):
    normal, _ = norm_parts(x_ref[...].astype(f32))
    normed = (normal * gain_ref[...] + beta_ref[...]).astype(bf16)
    normed_ref[...] = normed
    out_ref[...] = (dot(normed, w_ref[...], ((1,), (0,))) + bias_ref[...]).astype(bf16)


def norm_project(tokens, gain, beta, weight, bias):
    rows, width = tokens.shape
    out = weight.shape[1]
    tile = min(rows, 256)
    whole = lambda shape: pl.BlockSpec(shape, lambda i: (0, 0))
    part = lambda cols: pl.BlockSpec((tile, cols), lambda i: (i, 0))
    return call(
        norm_project_body,
        grid=(rows // tile,),
        in_specs=[part(width), whole((1, width)), whole((1, width)), whole(weight.shape), whole((1, out))],
        out_specs=[part(width), part(out)],
        out_shape=[jax.ShapeDtypeStruct((rows, width), bf16), jax.ShapeDtypeStruct((rows, out), bf16)],
        cost_estimate=pl.CostEstimate(
            flops=2 * rows * width * out, bytes_accessed=4 * rows * width + 2 * out * (rows + width), transcendentals=0
        ),
    )(tokens, gain, beta, weight, bias)


def tile_scores(query, key, slope, first, ids_col, ids_row, score_scale):
    scores = dot(query, key, ((1,), (1,))) * (score_scale * LOG2E)
    shape = scores.shape
    apart = lax.broadcasted_iota(jnp.int32, shape, 0) + first - lax.broadcasted_iota(jnp.int32, shape, 1)
    scores = scores - slope * jnp.abs(apart).astype(f32)
    return jnp.where(ids_row <= ids_col, scores, -1e30)


def attend_body(score_scale, heads, slope_ref, idc_ref, idr_ref, qkv_ref, ctx_ref, lse_ref):
    blocks, _, span, _ = qkv_ref.shape
    length = blocks * span
    cols = heads * HEAD_DIM
    step = BLOCK // span

    def piece(low, high, at):
        return qkv_ref[low:high, 0, :, at : at + HEAD_DIM].reshape((high - low) * span, HEAD_DIM)

    for head in range(heads):
        at = head * HEAD_DIM
        for t in range(length // BLOCK):
            top = min(blocks, (t + 2) * step)
            rows = slice(t * BLOCK, (t + 1) * BLOCK)
            scores = tile_scores(
                piece(t * step, (t + 1) * step, at),
                piece(0, top, cols + at),
                slope_ref[0, head] * LOG2E,
                t * BLOCK,
                idc_ref[0, rows],
                idr_ref[0, :, : top * span],
                score_scale,
            )
            row_max = jnp.max(scores, axis=-1, keepdims=True)
            exponent = jnp.exp2(scores - row_max)
            total = jnp.sum(exponent, axis=-1, keepdims=True)
            probs = (exponent * (1.0 / total)).astype(bf16)
            context = dot(probs, piece(0, top, 2 * cols + at), ((1,), (0,)))
            ctx_ref[t * step : (t + 1) * step, 0, :, at : at + HEAD_DIM] = context.astype(bf16).reshape(
                step, span, HEAD_DIM
            )
            lse_ref[0, rows, head : head + 1] = row_max + jnp.log2(total)


def attend_back_body(score_scale, heads, slope_ref, idc_ref, idr_ref, qkv_ref, grad_ref, lse_ref, out_ref, gk_ref, gv_ref):
    blocks, _, span, _ = qkv_ref.shape
    length = blocks * span
    cols = heads * HEAD_DIM
    step = BLOCK // span

    def piece(ref, low, high, at):
        return ref[low:high, 0, :, at : at + HEAD_DIM].reshape((high - low) * span, HEAD_DIM)

    def put(low, high, at, value):
        out_ref[low:high, 0, :, at : at + HEAD_DIM] = value.astype(bf16).reshape(high - low, span, HEAD_DIM)

    for head in range(heads):
        at = head * HEAD_DIM
        gk_ref[...] = jnp.zeros_like(gk_ref)
        gv_ref[...] = jnp.zeros_like(gv_ref)
        for t in range(length // BLOCK):
            top = min(blocks, (t + 2) * step)
            rows = slice(t * BLOCK, (t + 1) * BLOCK)
            query = piece(qkv_ref, t * step, (t + 1) * step, at)
            key = piece(qkv_ref, 0, top, cols + at)
            grad = piece(grad_ref, t * step, (t + 1) * step, at)
            scores = tile_scores(
                query,
                key,
                slope_ref[0, head] * LOG2E,
                t * BLOCK,
                idc_ref[0, rows],
                idr_ref[0, :, : top * span],
                score_scale,
            )
            probs = jnp.exp2(scores - lse_ref[0, rows, head : head + 1])
            grad_probs = dot(grad, piece(qkv_ref, 0, top, 2 * cols + at), ((1,), (1,)))
            total = jnp.sum(probs * grad_probs, axis=-1, keepdims=True)
            grad_scores = (probs * (grad_probs - total) * score_scale).astype(bf16)
            put(t * step, (t + 1) * step, at, dot(grad_scores, key, ((1,), (0,))))
            gk_ref[: top * span] += dot(grad_scores, query, ((0,), (0,)))
            gv_ref[: top * span] += dot(probs.astype(bf16), grad, ((0,), (0,)))
        put(0, blocks, cols + at, gk_ref[...])
        put(0, blocks, 2 * cols + at, gv_ref[...])


def attention_specs(blocks, span, cols, length, heads):
    split = lambda width: pl.BlockSpec((blocks, 1, span, width), lambda s: (0, s, 0, 0))
    return (
        pl.BlockSpec(memory_space=pltpu.SMEM),
        pl.BlockSpec((1, length, 1), lambda s: (s, 0, 0)),
        pl.BlockSpec((1, 1, length), lambda s: (s, 0, 0)),
        split(3 * cols),
        split(cols),
        pl.BlockSpec((1, length, heads), lambda s: (s, 0, 0)),
    )


def attend(slopes, ids, qkv, score_scale):
    blocks, seqs, span, width = qkv.shape
    length, cols = blocks * span, width // 3
    heads = cols // HEAD_DIM
    smem, idc, idr, three, one, lse = attention_specs(blocks, span, cols, length, heads)
    return call(
        lambda *refs: attend_body(score_scale, heads, *refs),
        grid=(seqs,),
        in_specs=[smem, idc, idr, three],
        out_specs=[one, lse],
        out_shape=[
            jax.ShapeDtypeStruct((blocks, seqs, span, cols), bf16),
            jax.ShapeDtypeStruct((seqs, length, heads), f32),
        ],
        cost_estimate=pl.CostEstimate(
            flops=4 * seqs * cols * length * length,
            bytes_accessed=8 * seqs * length * cols,
            transcendentals=seqs * heads * length * length,
        ),
    )(slopes, ids[:, :, None], ids[:, None, :], qkv)


def attend_back(slopes, ids, qkv, grad, stats, score_scale):
    blocks, seqs, span, width = qkv.shape
    length, cols = blocks * span, width // 3
    heads = cols // HEAD_DIM
    smem, idc, idr, three, one, lse = attention_specs(blocks, span, cols, length, heads)
    return call(
        lambda *refs: attend_back_body(score_scale, heads, *refs),
        grid=(seqs,),
        in_specs=[smem, idc, idr, three, one, lse],
        out_specs=three,
        out_shape=jax.ShapeDtypeStruct(qkv.shape, bf16),
        scratch_shapes=[pltpu.VMEM((length, HEAD_DIM), f32)] * 2,
        cost_estimate=pl.CostEstimate(
            flops=10 * seqs * cols * length * length,
            bytes_accessed=14 * seqs * length * cols,
            transcendentals=seqs * heads * length * length,
        ),
    )(slopes, ids[:, :, None], ids[:, None, :], qkv, grad, stats)


def norm_one_back_body(g_ref, w_ref, x_ref, out_ref, gain_ref, beta_ref):
    grad = dot(g_ref[...], w_ref[...], ((1,), (1,)))
    normal, _ = norm_parts(x_ref[...].astype(f32))
    out_ref[...] = grad.astype(bf16)

    @pl.when(pl.program_id(0) == 0)
    def _():
        gain_ref[...] = jnp.zeros_like(gain_ref)
        beta_ref[...] = jnp.zeros_like(beta_ref)

    gain_ref[...] += jnp.sum(grad * normal, axis=0, keepdims=True)
    beta_ref[...] += jnp.sum(grad, axis=0, keepdims=True)


def norm_one_back(grad_qkv, weight, tokens):
    rows, width = tokens.shape
    inner = weight.shape[1]
    tile = min(rows, 256)
    whole = lambda shape: pl.BlockSpec(shape, lambda i: (0, 0))
    part = lambda cols: pl.BlockSpec((tile, cols), lambda i: (i, 0))
    return call(
        norm_one_back_body,
        grid=(rows // tile,),
        in_specs=[part(inner), whole(weight.shape), part(width)],
        out_specs=[part(width), whole((1, width)), whole((1, width))],
        out_shape=[
            jax.ShapeDtypeStruct((rows, width), bf16),
            jax.ShapeDtypeStruct((1, width), f32),
            jax.ShapeDtypeStruct((1, width), f32),
        ],
        cost_estimate=pl.CostEstimate(
            flops=2 * rows * width * inner, bytes_accessed=4 * rows * width + 2 * inner * (rows + width), transcendentals=0
        ),
    )(grad_qkv, weight, tokens)


def on_device(
    inputs,
    block_ids,
    gain_one,
    beta_one,
    w_qkv,
    bias_query,
    bias_value,
    w_out,
    bias_out,
    gain_two,
    beta_two,
    w_up,
    bias_up,
    w_down,
    bias_down,
    cotangent,
):
    seqs, span, width = inputs.shape
    rows = seqs * span
    n_dp = lax.axis_size("dp")
    n_line = lax.axis_size(LINE)
    length = span * n_line
    share = w_qkv.shape[0]
    feed = w_up.shape[1]
    feed_own = feed // n_dp
    cols = width // n_line
    heads = cols // HEAD_DIM
    score_scale = HEAD_DIM ** (-0.5)
    line_at = lax.axis_index(LINE)

    small = jnp.stack(
        [gain_one, beta_one, bias_query, bias_value, bias_out, gain_two, beta_two, bias_down]
    ).reshape(-1)
    small = jnp.concatenate([small, bias_up])
    small_all = lax.all_gather(small, ALL, axis=0, tiled=False).astype(f32)
    vectors = small_all[:, : 8 * share].reshape(-1, 8, share).transpose(1, 0, 2).reshape(8, width)
    gain1, beta1, biasq, biasv, biaso, gain2, beta2, biasd = [vectors[i][None] for i in range(8)]
    up_bias_all = small_all[:, 8 * share :].reshape(n_dp, 1, feed_own)
    up_bias = lax.dynamic_index_in_dim(up_bias_all, lax.axis_index("dp"), 0, keepdims=False)
    biasq_own = lax.dynamic_slice_in_dim(biasq, line_at * cols, cols, 1)
    biasv_own = lax.dynamic_slice_in_dim(biasv, line_at * cols, cols, 1)

    qkv_send = w_qkv.reshape(share, 3, n_line, cols).transpose(2, 0, 1, 3).reshape(n_line, share, 3 * cols)
    qkv_got = lax.all_to_all(qkv_send, LINE, split_axis=0, concat_axis=0, tiled=True)
    qkv_own = gather_dp_rows(qkv_got.reshape(n_line * share, 3 * cols))
    tokens_line = lax.all_gather(inputs, LINE, axis=0, tiled=False)
    ids_line = lax.all_gather(block_ids.astype(bf16), LINE, axis=0, tiled=False)

    out_full = lax.all_gather(w_out, ALL, axis=0, tiled=True)
    up_send = w_up.reshape(share, n_dp, feed_own).transpose(1, 0, 2)
    up_got = lax.all_to_all(up_send, "dp", split_axis=0, concat_axis=0, tiled=True)
    up_own = (
        lax.all_gather(up_got, LINE, axis=0, tiled=False)
        .transpose(1, 0, 2, 3)
        .reshape(width, feed_own)
    )
    down_own = lax.all_gather(w_down, LINE, axis=0, tiled=True)

    tokens_line = tokens_line.reshape(n_line * rows, width)
    bias_row = jnp.concatenate([biasq_own, jnp.zeros_like(biasq_own), biasv_own], axis=1)
    normed_one, qkv = norm_project(tokens_line, gain1, beta1, qkv_own, bias_row)
    qkv = qkv.reshape(n_line, seqs, span, 3 * cols)
    ids = ids_line.astype(f32).transpose(1, 0, 2).reshape(seqs, length)
    numbers = (line_at * heads + jnp.arange(heads)).astype(f32)
    slopes = jnp.exp2(-8.0 * (numbers + 1.0) / (n_line * heads))[None]
    context_own, stats = attend(slopes, ids, qkv, score_scale)
    context_own = context_own.reshape(n_line, rows, cols)
    context = (
        lax.all_to_all(context_own, LINE, split_axis=0, concat_axis=0, tiled=True)
        .transpose(1, 0, 2)
        .reshape(rows, width)
    )

    tokens = inputs.astype(f32).reshape(rows, width)
    residual = tokens + dot(context, out_full, ((1,), (0,))) + biaso
    normal_two, scale_two = norm_parts(residual)
    normed_two = (normal_two * gain2 + beta2).astype(bf16)

    grad_out = cotangent.reshape(rows, width)
    grad_out_dp = gather_dp(grad_out).reshape(n_dp * rows, width)
    normed_two_dp = gather_dp(normed_two).reshape(n_dp * rows, width)
    hidden = dot(normed_two_dp, up_own, ((1,), (0,))) + up_bias
    activated_f, gelu_slope = gelu_both(hidden)
    activated = activated_f.astype(bf16)
    grad_hidden_f = dot(grad_out_dp, down_own, ((1,), (1,))) * gelu_slope
    grad_hidden = grad_hidden_f.astype(bf16)
    grad_normed_two = scatter_dp(dot(grad_hidden, up_own, ((1,), (1,))).reshape(n_dp, rows, width))
    feed_out = scatter_dp(dot(activated, down_own, ((1,), (0,))).reshape(n_dp, rows, width))
    outputs = (residual + feed_out + biasd).astype(bf16).reshape(seqs, span, width)

    grad_down = dot(activated, grad_out_dp, ((0,), (0,))).astype(bf16)
    grad_w_down = lax.psum_scatter(grad_down, LINE, scatter_dimension=0, tiled=True).astype(f32)
    grad_up = dot(normed_two_dp, grad_hidden, ((0,), (0,))).astype(bf16)
    grad_up = grad_up.reshape(n_dp, n_line, share, feed_own).transpose(1, 0, 2, 3).reshape(width, feed_own)
    grad_up = lax.psum_scatter(grad_up, LINE, scatter_dimension=0, tiled=True).reshape(n_dp, share, feed_own)
    grad_w_up = (
        lax.all_to_all(grad_up, "dp", split_axis=0, concat_axis=0, tiled=True)
        .transpose(1, 0, 2)
        .reshape(share, feed)
        .astype(f32)
    )
    bias_up_part = jnp.sum(grad_hidden.astype(f32), axis=0)

    grad_out_f = grad_out.astype(f32)
    grad_residual = grad_out_f + norm_back(grad_normed_two, gain2, normal_two, scale_two)
    gain2_part = jnp.sum(grad_normed_two * normal_two, axis=0)
    beta2_part = jnp.sum(grad_normed_two, axis=0)
    biasd_part = jnp.sum(grad_out_f, axis=0)
    biaso_part = jnp.sum(grad_residual, axis=0)

    grad_branch = grad_residual.astype(bf16)
    grad_context = dot(grad_branch, out_full, ((1,), (1,))).astype(bf16)
    grad_context = lax.all_to_all(
        grad_context.reshape(rows, n_line, cols).transpose(1, 0, 2), LINE, split_axis=0, concat_axis=0, tiled=True
    ).reshape(n_line, seqs, span, cols)
    grad_out_w = dot(context, grad_branch, ((0,), (0,))).astype(bf16)
    grad_w_out = lax.psum_scatter(grad_out_w, ALL, scatter_dimension=0, tiled=True).astype(f32)

    grad_qkv = attend_back(slopes, ids, qkv, grad_context, stats, score_scale).reshape(n_line * rows, 3 * cols)

    grad_normed_part, gain1_part, beta1_part = norm_one_back(grad_qkv, qkv_own, tokens_line)
    gain1_part, beta1_part = gain1_part[0], beta1_part[0]
    grad_normed_one = lax.psum_scatter(
        grad_normed_part, LINE, scatter_dimension=0, tiled=True
    ).astype(f32)
    normal_one, scale_one = norm_parts(tokens)
    grad_inputs = grad_residual + norm_back(grad_normed_one, gain1, normal_one, scale_one)
    bias_qkv_part = jnp.sum(grad_qkv.astype(f32), axis=0)

    grad_qkv_w = dot(normed_one, grad_qkv, ((0,), (0,))).astype(bf16)
    grad_qkv_w = lax.psum_scatter(grad_qkv_w, "dp", scatter_dimension=0, tiled=True)
    grad_w_qkv = (
        lax.all_to_all(grad_qkv_w.reshape(n_line, share, 3 * cols), LINE, split_axis=0, concat_axis=0, tiled=True)
        .reshape(n_line, share, 3, cols)
        .transpose(1, 2, 0, 3)
        .reshape(share, 3 * width)
        .astype(f32)
    )

    def spread(own, count, at):
        return lax.dynamic_update_slice_in_dim(jnp.zeros((count,) + own.shape, f32), own[None], at, 0)

    biasq_part = spread(bias_qkv_part[:cols], n_line, line_at).reshape(-1)
    biasv_part = spread(bias_qkv_part[2 * cols :], n_line, line_at).reshape(-1)
    bias_up_whole = spread(bias_up_part, n_dp, lax.axis_index("dp")).reshape(-1)
    parts = jnp.stack(
        [biasq_part, biasv_part, biaso_part, gain1_part, beta1_part, biasd_part, gain2_part, beta2_part]
    )
    n_all = n_dp * n_line
    parts = parts.reshape(8, n_all, share).transpose(1, 0, 2).reshape(n_all, 8 * share)
    parts = jnp.concatenate([parts, bias_up_whole.reshape(n_all, -1)], axis=1)
    parts = lax.all_to_all(parts, ALL, split_axis=0, concat_axis=0, tiled=True)
    own = jnp.sum(parts, axis=0)
    vec = own[: 8 * share].reshape(8, share)

    return (
        outputs,
        grad_inputs.reshape(seqs, span, width),
        grad_w_qkv,
        vec[0],
        vec[1],
        grad_w_out,
        vec[2],
        vec[3],
        vec[4],
        grad_w_up,
        own[8 * share :],
        grad_w_down,
        vec[5],
        vec[6],
        vec[7],
    )


def solution(mesh):
    tokens, ids, matrix, vector = P("dp", LINE, None), P("dp", LINE), P(ALL, None), P(ALL)
    placed = (
        tokens,
        ids,
        vector,
        vector,
        matrix,
        vector,
        vector,
        matrix,
        vector,
        vector,
        vector,
        matrix,
        vector,
        matrix,
        vector,
        tokens,
    )
    given = (
        tokens,
        tokens,
        matrix,
        vector,
        vector,
        matrix,
        vector,
        vector,
        vector,
        matrix,
        vector,
        matrix,
        vector,
        vector,
        vector,
    )
    return jax.shard_map(on_device, mesh=mesh, in_specs=placed, out_specs=given, check_vma=False)
```

```python
import jax
import jax.numpy as jnp
from jax import lax
from jax.experimental import pallas as pl
from jax.experimental.pallas import tpu as pltpu
from jax.sharding import PartitionSpec as P

HEAD_DIM = 128
EPSILON = 1e-05
ALL = ("dp", "seq", "fsdp")
LINE = ("seq", "fsdp")
FAR = ((0, 2), (1, 3))
f32 = jnp.float32
bf16 = jnp.bfloat16


def dot(left, right, dims):
    return lax.dot_general(left, right, (dims, ((), ())), preferred_element_type=f32)


def norm_parts(values):
    average = jnp.mean(values, axis=-1, keepdims=True)
    centered = values - average
    variance = jnp.mean(centered * centered, axis=-1, keepdims=True)
    scale = lax.rsqrt(variance + EPSILON)
    return centered * scale, scale


def norm_back(grad, gain, normal, scale):
    scaled = grad * gain
    return scale * (
        scaled
        - jnp.mean(scaled, axis=-1, keepdims=True)
        - normal * jnp.mean(scaled * normal, axis=-1, keepdims=True)
    )


def gelu_both(hidden):
    root = (2.0 / jnp.pi) ** 0.5
    square = hidden * hidden
    tanh = jnp.tanh(root * (hidden + 0.044715 * hidden * square))
    half = 0.5 * (1.0 + tanh)
    slope = half + 0.5 * hidden * (1.0 - tanh * tanh) * root * (1.0 + 3 * 0.044715 * square)
    return hidden * half, slope


def swap(value, axis, mask):
    return lax.ppermute(value, axis, [(i, i ^ mask) for i in range(lax.axis_size(axis))])


def hop(value, pairs):
    return lax.ppermute(value, "seq", list(pairs))


def in_plane():
    return lax.axis_size("dp") == 4 and lax.axis_size("seq") == 4 and lax.axis_size("fsdp") == 2


def after(value, *earlier):
    return lax.optimization_barrier((value,) + earlier)[0]


def assemble(shape, parts, copies, scalars):
    def body(s_ref, *refs):
        out, sems = refs[len(parts)], refs[len(parts) + 1]
        flights = []
        for number, (part, source, target) in enumerate(copies):
            flight = pltpu.make_async_copy(refs[part].at[source], out.at[target(s_ref)], sems.at[number])
            flight.start()
            flights.append(flight)
        for flight in flights:
            flight.wait()

    size = 2 * shape[-1]
    for extent in shape[:-1]:
        size *= extent
    return call(
        body,
        in_specs=[pl.BlockSpec(memory_space=pltpu.SMEM)] + [pl.BlockSpec(memory_space=pl.ANY)] * len(parts),
        out_specs=pl.BlockSpec(memory_space=pltpu.VMEM),
        out_shape=jax.ShapeDtypeStruct(shape, bf16),
        scratch_shapes=[pltpu.SemaphoreType.DMA((len(copies),))],
        cost_estimate=cost(flops=0, bytes_accessed=2 * size, transcendentals=0),
    )(jnp.stack(scalars).astype(jnp.int32), *parts)


def pick(whole, at, axis=0):
    return lax.dynamic_index_in_dim(whole, at, axis, keepdims=False)


def unxor(value, axis, at):
    shape = value.shape
    bit = 1
    while bit < shape[axis]:
        pairs = value.reshape(shape[:axis] + (-1, 2, bit) + shape[axis + 1 :])
        other = jnp.flip(pairs, axis + 1).reshape(shape)
        value = jnp.where((at & bit) != 0, other, value)
        bit *= 2
    return value


def scatter_one(parts):
    half = parts[0].shape[0] // 2
    low = parts[3].astype(bf16)
    return swap(low[:half], "dp", 1), swap(low[half:], "dp", 2)


def scatter_mid(parts, got):
    half = parts[0].shape[0] // 2
    one, two = parts[1].astype(f32), parts[2].astype(f32)
    two = jnp.concatenate([two[:half] + got[0].astype(f32), two[half:]], axis=0).astype(bf16)
    one = jnp.concatenate([one[:half], one[half:] + got[1].astype(f32)], axis=0).astype(bf16)
    return one, two


def scatter_send(mid):
    return swap(mid[0], "dp", 1), swap(mid[1], "dp", 2)


def scatter_two(parts, got):
    return scatter_send(scatter_mid(parts, got))


def scatter_sum(parts, got):
    return parts[0].astype(f32) + got[0].astype(f32) + got[1].astype(f32)


class Plane:
    def __init__(self, share, feed, width):
        self.dp, self.seq, self.core = [lax.axis_index(axis) for axis in ALL]
        self.near, self.far = self.seq & 1, self.seq >> 1
        self.share, self.feed_width, self.width = share, feed, width
        self.block = feed // 32

    def begin(self, send, inputs, weights, dy):
        w_out, w_up, self.w_down = weights
        self.dy = dy
        share, rows = self.share, dy.shape[0]
        half = rows // 2
        halves = send.reshape(4, 2, share + 16, -1)
        got = swap(pick(halves, 1 - self.core, 1), "fsdp", 1)
        both = jnp.stack([pick(halves, self.core, 1), got], axis=1)
        dy_one, dy_two = swap(dy, "dp", 1), swap(dy, "dp", 2)
        whole = w_up.reshape(share, 4, 2, 2, 2 * self.block)
        split = lambda near: pick(whole, near, 3).transpose(1, 0, 2, 3).reshape(4, share, 4 * self.block)
        near = swap(split(1 - self.near), "seq", 1)
        out_line = lax.all_gather(w_out, "seq", axis=0, tiled=False)
        block = [pick(both, self.seq)] + [swap(pick(both, self.seq ^ k), "seq", k) for k in (1, 2, 3)]
        block = after(jnp.stack(block), dy_one, dy_two, near)
        line = lax.all_gather(after(inputs, block), LINE, axis=0, tiled=False)

        one, two = swap(block, "dp", 1), swap(block, "dp", 2)
        dy_top = swap(after(dy_two[:half], block), "dp", 1)
        dy_low = swap(after(dy_one[half:], block), "dp", 2)
        self.dy_first = jnp.concatenate([dy, dy_one, dy_two, dy_top, dy_low], axis=0)
        one, two, dy_top, dy_low = lax.optimization_barrier((one, two, dy_top, dy_low))

        top, low = swap(two[:2], "dp", 1), swap(one[2:], "dp", 2)
        columns = jnp.stack([split(self.near), near], axis=1)
        self.up_rows = jnp.stack(
            [pick(columns, self.dp)] + [swap(after(pick(columns, self.dp ^ k), one), "dp", k) for k in (1, 2, 3)]
        )
        self.out_mine = out_line
        self.out_one, self.out_two = [swap(after(out_line, top, low), "dp", k) for k in (1, 2)]
        line = after(line, self.up_rows, self.out_one, self.out_two)

        copies = []
        for k in range(4):
            for z in range(4):
                for f in range(2):
                    part, at = (k, z) if k < 3 else (3 + z // 2, z % 2)
                    target = lambda s, k=k, z=z, f=f: (s[0] ^ k, s[1] ^ z, s[2] ^ f)
                    copies.append((part, (at, f, slice(0, share)), target))
        parts = [block, one, two, top, low]
        shape = (4, 4, 2, share, block.shape[3])
        qkv_own = assemble(shape, parts, copies, [self.dp, self.seq, self.core]).reshape(self.width, -1)
        small = [block[:, :, share], one[:, :, share], two[:, :, share]]
        small.append(jnp.concatenate([top[:, :, share], low[:, :, share]], axis=0))
        small = unxor(unxor(unxor(jnp.stack(small), 0, self.dp), 1, self.seq), 2, self.core).reshape(32, -1)
        ids = unxor(unxor(block[:, :, share + 1, :rows], 0, self.seq), 1, self.core).reshape(8, rows)
        return line, qkv_own, small, ids

    def tokens_there(self, tokens):
        self.dy_near = swap(after(self.dy, tokens), "seq", 1)
        down = lax.all_gather(after(self.w_down, tokens), "seq", axis=0, tiled=False, axis_index_groups=FAR)
        up = lax.all_gather(after(self.up_rows, tokens), "seq", axis=0, tiled=False, axis_index_groups=FAR)
        self.gathered = (up, down)

    def out_start(self, qkv, context):
        top, low = swap(self.out_two[:2], "dp", 1), swap(self.out_one[2:], "dp", 2)
        parts = [self.out_mine, self.out_one, self.out_two, jnp.concatenate([top, low], axis=0)]
        self.out_mine = jnp.stack(parts)
        self.dy_one, self.dy_two = [swap(after(self.dy_near, context), "dp", k) for k in (1, 2)]
        return after(context, top, low)

    def out(self, context):
        mine = self.out_mine
        other = swap(mine, "fsdp", 1)
        context = after(context, self.dy_one, self.dy_two, self.gathered[1])
        copies = [
            (f, (k, z), lambda s, f=f, k=k, z=z: (s[0] ^ k, z, s[1] ^ f))
            for f in range(2)
            for k in range(4)
            for z in range(4)
        ]
        whole = assemble(
            (4, 4, 2, self.share, self.width), [mine, other], copies, [self.dp, self.core]
        )
        return whole.reshape(self.width, self.width), context

    def gather(self, normed):
        half = normed.shape[0] // 2
        near, dy_one, dy_two = self.dy_near, self.dy_one, self.dy_two
        dy_top, dy_low = swap(dy_two[:half], "dp", 1), swap(dy_one[half:], "dp", 2)
        dy_second = jnp.concatenate([near, dy_one, dy_two, dy_top, dy_low], axis=0)
        normed = after(normed, dy_top, dy_low)
        other = swap(normed, "seq", 1)
        one, two = swap(normed, "dp", 1), swap(normed, "dp", 2)
        halves = lax.optimization_barrier((two[:half], one[half:]))
        top, low = swap(halves[0], "dp", 1), swap(halves[1], "dp", 2)
        up, down = [after(part, *halves) for part in self.gathered]
        up_other, down_other = swap(up, "fsdp", 1), swap(down, "fsdp", 1)
        first = jnp.concatenate([normed, one, two, top, low], axis=0)
        other_one, other_two = [swap(after(other, top, low), "dp", k) for k in (1, 2)]
        other_top, other_low = swap(other_two[:half], "dp", 1), swap(other_one[half:], "dp", 2)
        second = jnp.concatenate([other, other_one, other_two, other_top, other_low], axis=0)
        copies = [(f, (far,), lambda s, far=far, f=f: (far, s[0] ^ f)) for far in range(2) for f in range(2)]
        shape = (2, 2, self.block, self.width)
        down = assemble(shape, [down, down_other], copies, [self.core]).reshape(4 * self.block, self.width)
        copies = [
            (f, (far, k, n), lambda s, far=far, f=f, k=k, n=n: (s[0] ^ k, far, s[1] ^ n, s[2] ^ f))
            for far in range(2)
            for f in range(2)
            for k in range(4)
            for n in range(2)
        ]
        shape = (4, 2, 2, 2, self.share, 4 * self.block)
        up = assemble(shape, [up, up_other], copies, [self.dp, self.near, self.core])
        return [first, second], [self.dy_first, dy_second], up.reshape(self.width, 4 * self.block), down

    def bias(self, table):
        return pick(pick(table.reshape(4, 2, 2, 2, -1), self.dp).transpose(1, 0, 2, 3), self.near).reshape(1, -1)

    def bias_spread(self, own):
        whole = jnp.zeros((4, 2, 2, 2, self.block), f32)
        own = own.reshape(1, 2, 1, 2, self.block)
        return lax.dynamic_update_slice(whole, own, (self.dp, 0, self.near, 0, 0)).reshape(-1)

    def feed(self, groups, dys, up, down, bias):
        own_act, own_gh, own_gn = feed_forward(groups[0], dys[0], up, down, bias)
        own_parts = jnp.split(own_gn, 4)
        own_one = scatter_one(own_parts)
        act, gh, gn = feed_forward(after(groups[1], *own_one), dys[1], up, down, bias)
        own_two = scatter_two(own_parts, own_one)
        parts = jnp.split(after(gn, *own_two), 4)
        mid = scatter_mid(parts, scatter_one(parts))
        two = scatter_send(mid)
        self.acts = after(jnp.concatenate([own_act, act], axis=0), *mid)
        ghs = after(jnp.concatenate([own_gh, gh], axis=0), *mid)
        grad_down = dot(self.acts, jnp.concatenate(dys, axis=0), ((0,), (0,))).astype(bf16)
        fed = dot(after(self.acts, grad_down), down, ((1,), (0,))).astype(bf16)
        self.fed = [fed.reshape(2, 4, -1, self.width)[:, k] for k in range(4)]
        whole = grad_down.reshape(2, 2, self.block, self.width)
        theirs = swap(pick(whole, 1 - self.core, 1), "fsdp", 1)
        grad_down = (pick(whole, self.core, 1).astype(f32) + after(theirs, fed).astype(f32)).astype(bf16)
        ghs = after(ghs, grad_down)
        grad_up = dot(jnp.concatenate(groups, axis=0), ghs, ((0,), (0,))).astype(bf16)
        whole = grad_up.reshape(4, 2, 2, 2, self.share, -1)
        theirs = swap(pick(whole, 1 - self.core, 3), "fsdp", 1)
        grad_up = (pick(whole, self.core, 3).astype(f32) + theirs.astype(f32)).astype(bf16)
        grad_up = grad_up.transpose(1, 0, 2, 3, 4)
        self.grad_down, rows = [
            lax.psum_scatter(
                grad.reshape(2 * self.block, self.width) if k == 0 else grad.reshape(self.width // 2, -1),
                "seq",
                scatter_dimension=0,
                tiled=True,
                axis_index_groups=FAR,
            )
            for k, grad in enumerate((grad_down, grad_up))
        ]
        self.grad_down = self.grad_down.astype(f32)
        self.up_rows = rows.reshape(4, 2, self.share, -1)
        other = scatter_sum(parts, two).astype(bf16)
        grad = scatter_sum(own_parts, own_two) + swap(other, "seq", 1).astype(f32)
        self.fed_one = scatter_one([after(part, other) for part in self.fed])
        self.grad_up = grad_up
        return after(grad, grad_down), ghs

    def before_exchange(self, grad_context):
        return after(grad_context, self.grad_up, *self.fed_one)

    def before_attention(self, got, sent, grad_out_w):
        fed_one = [after(part, sent) for part in self.fed_one]
        self.fed_two = scatter_two(self.fed, fed_one)
        whole = grad_out_w.reshape(4, 4, 2, self.share, self.width)
        theirs = swap(pick(whole, 1 - self.core, 2), "fsdp", 1)
        whole = (pick(whole, self.core, 2).astype(f32) + theirs.astype(f32)).astype(bf16)
        self.out_parts = [pick(whole, self.dp ^ k) for k in range(4)]
        return after(got, whole)

    def before_norm(self, grad_qkv):
        own, other = scatter_sum(self.fed, self.fed_two)
        self.feed_out = own + swap(other.astype(bf16), "seq", 1).astype(f32)
        self.out_one = scatter_one(self.out_parts)
        return after(grad_qkv, *self.fed_two, *self.out_one)

    def last(self, normed, grad_qkv):
        grad = dot(normed, grad_qkv, ((0,), (0,))).astype(bf16)
        out_two = scatter_two(self.out_parts, self.out_one)
        parts = [pick(grad.reshape(4, -1, grad.shape[1]), self.dp ^ k) for k in range(4)]
        parts[3] = after(parts[3], *out_two)
        one = scatter_one(parts)
        line = scatter_sum(self.out_parts, out_two).reshape(2, 2, self.share, self.width)
        away = pick(line, 1 - self.far)
        away = away + hop(away.astype(bf16), ((0, 1), (3, 2))).astype(f32)
        line = pick(line, self.far) + hop(away.astype(bf16), ((1, 2), (2, 1))).astype(f32)
        grad_out = pick(line, self.near) + swap(pick(line, 1 - self.near).astype(bf16), "seq", 1).astype(f32)
        two = scatter_two(parts, one)
        grad_up = self.up_back_end(after(self.up_rows, *one))
        return scatter_sum(parts, two), grad_out, grad_up, self.grad_down

    def up_back_end(self, rows):
        parts = [pick(rows, self.dp)] + [swap(pick(rows, self.dp ^ k), "dp", k) for k in (1, 2, 3)]
        parts = jnp.stack(parts)
        pair = [pick(parts, self.near, 1), swap(pick(parts, 1 - self.near, 1), "seq", 1)]
        wide = 2 * self.block

        def body(s_ref, own_ref, other_ref, out_ref):
            for n, ref in enumerate((own_ref, other_ref)):
                for k in range(4):
                    for far in range(2):
                        at = ((s_ref[0] ^ k) * 4 + far * 2 + (s_ref[1] ^ n)) * wide
                        piece = ref[k, :, far * wide : (far + 1) * wide]
                        out_ref[:, pl.ds(pl.multiple_of(at, wide), wide)] = piece.astype(f32)

        return call(
            body,
            in_specs=[pl.BlockSpec(memory_space=pltpu.SMEM)] + [pl.BlockSpec(memory_space=pltpu.VMEM)] * 2,
            out_specs=pl.BlockSpec(memory_space=pltpu.VMEM),
            out_shape=jax.ShapeDtypeStruct((self.share, self.feed_width), f32),
            cost_estimate=cost(flops=0, bytes_accessed=6 * self.share * self.feed_width, transcendentals=0),
        )(jnp.stack([self.dp, self.near]).astype(jnp.int32), *pair)


class General:
    def __init__(self, share, feed, width):
        self.dp, self.n_dp, self.line = lax.axis_index("dp"), lax.axis_size("dp"), lax.axis_size(LINE)
        self.share, self.feed_width = share, feed

    def begin(self, send, inputs, weights, dy):
        self.w_out, self.w_up, self.w_down = weights
        self.dy = dy
        line = lax.all_gather(inputs, LINE, axis=0, tiled=False)
        got = lax.all_to_all(send, LINE, split_axis=0, concat_axis=0, tiled=True)
        whole = lax.all_gather(got, "dp", axis=0, tiled=True)
        share = self.share
        ids = got[:, share + 1, : dy.shape[0]]
        return line, whole[:, :share].reshape(-1, got.shape[2]), whole[:, share], ids

    def tokens_there(self, tokens):
        pass

    def out_start(self, qkv, context):
        return context

    def out(self, context):
        return lax.all_gather(self.w_out, ALL, axis=0, tiled=True), context

    def gather(self, normed):
        groups = [
            jnp.split(lax.all_gather(block, "dp", axis=0, tiled=True), self.groups()) for block in (normed, self.dy)
        ]
        sent = self.w_up.reshape(self.share, self.n_dp, -1).transpose(1, 0, 2)
        rows = lax.all_to_all(sent, "dp", split_axis=0, concat_axis=0, tiled=True)
        rows = lax.all_gather(rows, LINE, axis=0, tiled=False).transpose(1, 0, 2, 3)
        up = rows.reshape(-1, self.feed_width // self.n_dp)
        return groups[0], groups[1], up, lax.all_gather(self.w_down, LINE, axis=0, tiled=True)

    def bias(self, table):
        return pick(table.reshape(self.n_dp, 1, -1), self.dp)

    def bias_spread(self, own):
        whole = jnp.zeros((self.n_dp, own.shape[0]), f32)
        return lax.dynamic_update_slice_in_dim(whole, own[None], self.dp, 0).reshape(-1)

    def groups(self):
        return 2 if self.n_dp % 2 == 0 else 1

    def scatter(self, groups):
        whole = jnp.concatenate(groups, axis=0)
        return lax.psum_scatter(whole, "dp", scatter_dimension=0, tiled=True).astype(f32)

    def feed(self, groups, dys, up, down, bias):
        own = self.feed_width // self.n_dp
        done = [feed_forward(x, dy, up, down, bias) for x, dy in zip(groups, dys)]
        acts, ghs = [jnp.concatenate([part[k] for part in done], axis=0) for k in range(2)]
        grad_down = dot(acts, jnp.concatenate(dys, axis=0), ((0,), (0,))).astype(bf16)
        self.grad_down = lax.psum_scatter(grad_down, LINE, scatter_dimension=0, tiled=True).astype(f32)
        rows = dot(jnp.concatenate(groups, axis=0), ghs, ((0,), (0,))).astype(bf16)
        rows = rows.reshape(self.n_dp, self.line, self.share, own).transpose(1, 0, 2, 3).reshape(-1, own)
        rows = lax.psum_scatter(rows, LINE, scatter_dimension=0, tiled=True).reshape(self.n_dp, self.share, own)
        rows = lax.all_to_all(rows, "dp", split_axis=0, concat_axis=0, tiled=True)
        self.grad_up = rows.transpose(1, 0, 2).reshape(self.share, self.feed_width).astype(f32)
        self.feed_out = self.scatter([dot(part[0], down, ((1,), (0,))).astype(bf16) for part in done])
        return self.scatter([part[2] for part in done]), ghs

    def before_exchange(self, grad_context):
        return grad_context

    def before_attention(self, got, sent, grad_out_w):
        self.grad_out = lax.psum_scatter(grad_out_w, ALL, scatter_dimension=0, tiled=True).astype(f32)
        return got

    def before_norm(self, grad_qkv):
        return grad_qkv

    def last(self, normed, grad_qkv):
        grad = dot(normed, grad_qkv, ((0,), (0,))).astype(bf16)
        grad = lax.psum_scatter(grad, "dp", scatter_dimension=0, tiled=True)
        return grad, self.grad_out, self.grad_up, self.grad_down


BLOCK = 256
LOG2E = 1.4426950408889634
VMEM_BYTES = 56 * 2**20


COST = 1000


def cost(flops, bytes_accessed, transcendentals):
    return pl.CostEstimate(
        flops=flops // COST, bytes_accessed=bytes_accessed // COST, transcendentals=transcendentals // COST
    )


def call(body, **options):
    return pl.pallas_call(
        body, compiler_params=pltpu.CompilerParams(vmem_limit_bytes=VMEM_BYTES), **options
    )


def norm_project_body(x_ref, gain_ref, beta_ref, w_ref, bias_ref, normed_ref, out_ref):
    normal, _ = norm_parts(x_ref[...].astype(f32))
    normed = (normal * gain_ref[...] + beta_ref[...]).astype(bf16)
    normed_ref[...] = normed
    out_ref[...] = (dot(normed, w_ref[...], ((1,), (0,))) + bias_ref[...]).astype(bf16)


def norm_project(tokens, gain, beta, weight, bias):
    rows, width = tokens.shape
    out = weight.shape[1]
    tile = min(rows, 256)
    whole = lambda shape: pl.BlockSpec(shape, lambda i: (0, 0))
    part = lambda cols: pl.BlockSpec((tile, cols), lambda i: (i, 0))
    return call(
        norm_project_body,
        grid=(rows // tile,),
        in_specs=[part(width), whole((1, width)), whole((1, width)), whole(weight.shape), whole((1, out))],
        out_specs=[part(width), part(out)],
        out_shape=[jax.ShapeDtypeStruct((rows, width), bf16), jax.ShapeDtypeStruct((rows, out), bf16)],
        cost_estimate=cost(
            flops=2 * rows * width * out, bytes_accessed=4 * rows * width + 2 * out * (rows + width), transcendentals=0
        ),
    )(tokens, gain, beta, weight, bias)


def tile_scores(query, key, slope, first, ids_col, ids_row, score_scale):
    scores = dot(query, key, ((1,), (1,))) * (score_scale * LOG2E)
    shape = scores.shape
    apart = lax.broadcasted_iota(jnp.int32, shape, 0) + first - lax.broadcasted_iota(jnp.int32, shape, 1)
    scores = scores - slope * jnp.abs(apart).astype(f32)
    return jnp.where(ids_row <= ids_col, scores, -1e30)


def attend_body(score_scale, heads, slope_ref, idc_ref, idr_ref, qkv_ref, ctx_ref, lse_ref):
    blocks, _, span, _ = qkv_ref.shape
    length = blocks * span
    cols = heads * HEAD_DIM
    step = BLOCK // span

    def piece(low, high, at):
        return qkv_ref[low:high, 0, :, at : at + HEAD_DIM].reshape((high - low) * span, HEAD_DIM)

    for head in range(heads):
        at = head * HEAD_DIM
        for t in range(length // BLOCK):
            top = min(blocks, (t + 2) * step)
            rows = slice(t * BLOCK, (t + 1) * BLOCK)
            scores = tile_scores(
                piece(t * step, (t + 1) * step, at),
                piece(0, top, cols + at),
                slope_ref[0, head] * LOG2E,
                t * BLOCK,
                idc_ref[0, rows],
                idr_ref[0, :, : top * span],
                score_scale,
            )
            row_max = jnp.max(scores, axis=-1, keepdims=True)
            exponent = jnp.exp2(scores - row_max)
            total = jnp.sum(exponent, axis=-1, keepdims=True)
            probs = (exponent * (1.0 / total)).astype(bf16)
            context = dot(probs, piece(0, top, 2 * cols + at), ((1,), (0,)))
            ctx_ref[t * step : (t + 1) * step, 0, :, at : at + HEAD_DIM] = context.astype(bf16).reshape(
                step, span, HEAD_DIM
            )
            lse_ref[0, rows, head : head + 1] = row_max + jnp.log2(total)


def attend_back_body(score_scale, heads, slope_ref, idc_ref, idr_ref, qkv_ref, grad_ref, lse_ref, out_ref, gk_ref, gv_ref):
    blocks, _, span, _ = qkv_ref.shape
    length = blocks * span
    cols = heads * HEAD_DIM
    step = BLOCK // span

    def piece(ref, low, high, at):
        return ref[low:high, 0, :, at : at + HEAD_DIM].reshape((high - low) * span, HEAD_DIM)

    def put(low, high, at, value):
        out_ref[low:high, 0, :, at : at + HEAD_DIM] = value.astype(bf16).reshape(high - low, span, HEAD_DIM)

    for head in range(heads):
        at = head * HEAD_DIM
        gk_ref[...] = jnp.zeros_like(gk_ref)
        gv_ref[...] = jnp.zeros_like(gv_ref)
        for t in range(length // BLOCK):
            top = min(blocks, (t + 2) * step)
            rows = slice(t * BLOCK, (t + 1) * BLOCK)
            query = piece(qkv_ref, t * step, (t + 1) * step, at)
            key = piece(qkv_ref, 0, top, cols + at)
            grad = piece(grad_ref, t * step, (t + 1) * step, at)
            scores = tile_scores(
                query,
                key,
                slope_ref[0, head] * LOG2E,
                t * BLOCK,
                idc_ref[0, rows],
                idr_ref[0, :, : top * span],
                score_scale,
            )
            probs = jnp.exp2(scores - lse_ref[0, rows, head : head + 1])
            grad_probs = dot(grad, piece(qkv_ref, 0, top, 2 * cols + at), ((1,), (1,)))
            total = jnp.sum(probs * grad_probs, axis=-1, keepdims=True)
            grad_scores = (probs * (grad_probs - total) * score_scale).astype(bf16)
            put(t * step, (t + 1) * step, at, dot(grad_scores, key, ((1,), (0,))))
            gk_ref[: top * span] += dot(grad_scores, query, ((0,), (0,)))
            gv_ref[: top * span] += dot(probs.astype(bf16), grad, ((0,), (0,)))
        put(0, blocks, cols + at, gk_ref[...])
        put(0, blocks, 2 * cols + at, gv_ref[...])


def attention_specs(blocks, span, cols, length, heads):
    split = lambda width: pl.BlockSpec((blocks, 1, span, width), lambda s: (0, s, 0, 0))
    return (
        pl.BlockSpec(memory_space=pltpu.SMEM),
        pl.BlockSpec((1, length, 1), lambda s: (s, 0, 0)),
        pl.BlockSpec((1, 1, length), lambda s: (s, 0, 0)),
        split(3 * cols),
        split(cols),
        pl.BlockSpec((1, length, heads), lambda s: (s, 0, 0)),
    )


def attend(slopes, ids, qkv, score_scale):
    blocks, seqs, span, width = qkv.shape
    length, cols = blocks * span, width // 3
    heads = cols // HEAD_DIM
    smem, idc, idr, three, one, lse = attention_specs(blocks, span, cols, length, heads)
    return call(
        lambda *refs: attend_body(score_scale, heads, *refs),
        grid=(seqs,),
        in_specs=[smem, idc, idr, three],
        out_specs=[one, lse],
        out_shape=[
            jax.ShapeDtypeStruct((blocks, seqs, span, cols), bf16),
            jax.ShapeDtypeStruct((seqs, length, heads), f32),
        ],
        cost_estimate=cost(
            flops=4 * seqs * cols * length * length,
            bytes_accessed=8 * seqs * length * cols,
            transcendentals=seqs * heads * length * length,
        ),
    )(slopes, ids[:, :, None], ids[:, None, :], qkv)


def attend_back(slopes, ids, qkv, grad, stats, score_scale):
    blocks, seqs, span, width = qkv.shape
    length, cols = blocks * span, width // 3
    heads = cols // HEAD_DIM
    smem, idc, idr, three, one, lse = attention_specs(blocks, span, cols, length, heads)
    return call(
        lambda *refs: attend_back_body(score_scale, heads, *refs),
        grid=(seqs,),
        in_specs=[smem, idc, idr, three, one, lse],
        out_specs=three,
        out_shape=jax.ShapeDtypeStruct(qkv.shape, bf16),
        scratch_shapes=[pltpu.VMEM((length, HEAD_DIM), f32)] * 2,
        cost_estimate=cost(
            flops=10 * seqs * cols * length * length,
            bytes_accessed=14 * seqs * length * cols,
            transcendentals=seqs * heads * length * length,
        ),
    )(slopes, ids[:, :, None], ids[:, None, :], qkv, grad, stats)


def norm_one_back_body(g_ref, w_ref, x_ref, out_ref, gain_ref, beta_ref):
    grad = dot(g_ref[...], w_ref[...], ((1,), (1,)))
    normal, _ = norm_parts(x_ref[...].astype(f32))
    out_ref[...] = grad.astype(bf16)

    @pl.when(pl.program_id(0) == 0)
    def _():
        gain_ref[...] = jnp.zeros_like(gain_ref)
        beta_ref[...] = jnp.zeros_like(beta_ref)

    gain_ref[...] += jnp.sum(grad * normal, axis=0, keepdims=True)
    beta_ref[...] += jnp.sum(grad, axis=0, keepdims=True)


def norm_one_back(grad_qkv, weight, tokens):
    rows, width = tokens.shape
    inner = weight.shape[1]
    tile = min(rows, 256)
    whole = lambda shape: pl.BlockSpec(shape, lambda i: (0, 0))
    part = lambda cols: pl.BlockSpec((tile, cols), lambda i: (i, 0))
    return call(
        norm_one_back_body,
        grid=(rows // tile,),
        in_specs=[part(inner), whole(weight.shape), part(width)],
        out_specs=[part(width), whole((1, width)), whole((1, width))],
        out_shape=[
            jax.ShapeDtypeStruct((rows, width), bf16),
            jax.ShapeDtypeStruct((1, width), f32),
            jax.ShapeDtypeStruct((1, width), f32),
        ],
        cost_estimate=cost(
            flops=2 * rows * width * inner, bytes_accessed=4 * rows * width + 2 * inner * (rows + width), transcendentals=0
        ),
    )(grad_qkv, weight, tokens)


def feed_body(x_ref, dy_ref, up_ref, down_ref, bias_ref, act_ref, gh_ref, gn_ref):
    up = up_ref[...]
    hidden = dot(x_ref[...], up, ((1,), (0,))) + bias_ref[...]
    grad = dot(dy_ref[...], down_ref[...], ((1,), (1,)))
    activated, slope = gelu_both(hidden)
    act_ref[...] = activated.astype(bf16)
    grad = (grad * slope).astype(bf16)
    gh_ref[...] = grad
    gn_ref[...] = dot(grad, up, ((1,), (1,))).astype(bf16)


def feed_forward(x, dy, up, down, bias):
    rows, width = x.shape
    feed = up.shape[1]
    tile = 256
    whole = lambda shape: pl.BlockSpec(shape, lambda i: (0, 0), pipeline_mode=pl.Buffered(1))
    part = lambda cols: pl.BlockSpec((tile, cols), lambda i: (i, 0))
    return call(
        feed_body,
        grid=(rows // tile,),
        in_specs=[part(width), part(width), whole(up.shape), whole(down.shape), whole(bias.shape)],
        out_specs=[part(feed), part(feed), part(width)],
        out_shape=[jax.ShapeDtypeStruct((rows, feed), bf16)] * 2 + [jax.ShapeDtypeStruct((rows, width), bf16)],
        cost_estimate=cost(
            flops=6 * rows * width * feed,
            bytes_accessed=6 * rows * width + 4 * feed * (rows + width),
            transcendentals=rows * feed,
        ),
    )(x, dy, up, down, bias)


def on_device(
    inputs,
    block_ids,
    gain_one,
    beta_one,
    w_qkv,
    bias_query,
    bias_value,
    w_out,
    bias_out,
    gain_two,
    beta_two,
    w_up,
    bias_up,
    w_down,
    bias_down,
    cotangent,
):
    seqs, span, width = inputs.shape
    rows = seqs * span
    n_dp = lax.axis_size("dp")
    n_line = lax.axis_size(LINE)
    length = span * n_line
    share = w_qkv.shape[0]
    feed = w_up.shape[1]
    cols = width // n_line
    heads = cols // HEAD_DIM
    score_scale = HEAD_DIM ** (-0.5)
    line_at = lax.axis_index(LINE)

    feeder = (Plane if in_plane() else General)(share, feed, width)

    vectors = jnp.stack([gain_one, beta_one, bias_query, bias_value, bias_out, gain_two, beta_two, bias_down])
    small = jnp.concatenate([vectors.reshape(-1), bias_up])
    extra = jnp.zeros((16, 3 * cols), bf16)
    extra = extra.at[0, : small.shape[0]].set(small)
    extra = extra.at[1, :rows].set(block_ids.astype(bf16).reshape(-1))
    qkv_send = w_qkv.reshape(share, 3, n_line, cols).transpose(2, 0, 1, 3).reshape(n_line, share, 3 * cols)
    extra = jnp.broadcast_to(extra[None], (n_line,) + extra.shape)
    qkv_send = jnp.concatenate([qkv_send, extra], axis=1)
    grad_out = cotangent.reshape(rows, width)
    tokens_line, qkv_own, small_all, ids = feeder.begin(qkv_send, inputs, (w_out, w_up, w_down), grad_out)
    ids = ids.astype(f32).reshape(n_line, seqs, span).transpose(1, 0, 2).reshape(seqs, length)
    small_all = small_all[:, : small.shape[0]].astype(f32)
    vectors = small_all[:, : 8 * share].reshape(-1, 8, share).transpose(1, 0, 2).reshape(8, width)
    gain1, beta1, biasq, biasv, biaso, gain2, beta2, biasd = [vectors[i][None] for i in range(8)]
    up_bias = feeder.bias(small_all[:, 8 * share :])
    biasq_own = lax.dynamic_slice_in_dim(biasq, line_at * cols, cols, 1)
    biasv_own = lax.dynamic_slice_in_dim(biasv, line_at * cols, cols, 1)

    tokens_line = tokens_line.reshape(n_line * rows, width)
    tokens_line, qkv_own, vectors = lax.optimization_barrier((tokens_line, qkv_own, vectors))
    feeder.tokens_there(tokens_line)
    bias_row = jnp.concatenate([biasq_own, jnp.zeros_like(biasq_own), biasv_own], axis=1)
    normed_one, qkv = norm_project(tokens_line, gain1, beta1, qkv_own, bias_row)
    qkv = qkv.reshape(n_line, seqs, span, 3 * cols)
    numbers = (line_at * heads + jnp.arange(heads)).astype(f32)
    slopes = jnp.exp2(-8.0 * (numbers + 1.0) / (n_line * heads))[None]
    context_own, stats = attend(slopes, ids, qkv, score_scale)
    context_own = context_own.reshape(n_line, rows, cols)
    context_own = feeder.out_start(qkv, context_own)
    context = lax.all_to_all(context_own, LINE, split_axis=0, concat_axis=0, tiled=True)
    out_full, context = feeder.out(context)
    context = context.transpose(1, 0, 2).reshape(rows, width)

    tokens = inputs.astype(f32).reshape(rows, width)
    residual = tokens + dot(context, out_full, ((1,), (0,))) + biaso
    normal_two, scale_two = norm_parts(residual)
    normed_two = (normal_two * gain2 + beta2).astype(bf16)

    normed_groups, grad_out_groups, up_own, down_own = feeder.gather(normed_two)
    grad_normed_two, grad_hidden = feeder.feed(normed_groups, grad_out_groups, up_own, down_own, up_bias)
    bias_up_part = jnp.sum(grad_hidden.astype(f32), axis=0)

    grad_out_f = grad_out.astype(f32)
    grad_residual = grad_out_f + norm_back(grad_normed_two, gain2, normal_two, scale_two)
    gain2_part = jnp.sum(grad_normed_two * normal_two, axis=0)
    beta2_part = jnp.sum(grad_normed_two, axis=0)
    biasd_part = jnp.sum(grad_out_f, axis=0)
    biaso_part = jnp.sum(grad_residual, axis=0)

    grad_branch = grad_residual.astype(bf16)
    grad_context = dot(grad_branch, out_full, ((1,), (1,))).astype(bf16)
    grad_context = grad_context.reshape(rows, n_line, cols).transpose(1, 0, 2)
    grad_context = feeder.before_exchange(grad_context)
    grad_branch = after(grad_branch, grad_context)
    sent = grad_context
    grad_context = lax.all_to_all(grad_context, LINE, split_axis=0, concat_axis=0, tiled=True)
    grad_out_w = dot(context, grad_branch, ((0,), (0,))).astype(bf16)
    grad_context = feeder.before_attention(grad_context, sent, grad_out_w).reshape(n_line, seqs, span, cols)
    grad_qkv = attend_back(slopes, ids, qkv, grad_context, stats, score_scale).reshape(n_line * rows, 3 * cols)
    grad_qkv = feeder.before_norm(grad_qkv)
    grad_normed_part, gain1_part, beta1_part = norm_one_back(grad_qkv, qkv_own, tokens_line)
    gain1_part, beta1_part = gain1_part[0], beta1_part[0]
    grad_normed_one = lax.psum_scatter(
        grad_normed_part, LINE, scatter_dimension=0, tiled=True
    ).astype(f32)
    normal_one, scale_one = norm_parts(tokens)
    grad_inputs = grad_residual + norm_back(grad_normed_one, gain1, normal_one, scale_one)
    bias_qkv_part = jnp.sum(grad_qkv.astype(f32), axis=0)

    grad_qkv_w, grad_w_out, grad_w_up, grad_w_down = feeder.last(normed_one, grad_qkv)
    grad_qkv_w = grad_qkv_w.astype(bf16)
    outputs = (residual + feeder.feed_out + biasd).astype(bf16).reshape(seqs, span, width)
    grad_w_qkv = (
        lax.all_to_all(grad_qkv_w.reshape(n_line, share, 3 * cols), LINE, split_axis=0, concat_axis=0, tiled=True)
        .reshape(n_line, share, 3, cols)
        .transpose(1, 2, 0, 3)
        .reshape(share, 3 * width)
        .astype(f32)
    )

    def spread(own, count, at):
        return lax.dynamic_update_slice_in_dim(jnp.zeros((count,) + own.shape, f32), own[None], at, 0)

    biasq_part = spread(bias_qkv_part[:cols], n_line, line_at).reshape(-1)
    biasv_part = spread(bias_qkv_part[2 * cols :], n_line, line_at).reshape(-1)
    bias_up_whole = feeder.bias_spread(bias_up_part)
    parts = jnp.stack(
        [biasq_part, biasv_part, biaso_part, gain1_part, beta1_part, biasd_part, gain2_part, beta2_part]
    )
    n_all = n_dp * n_line
    parts = parts.reshape(8, n_all, share).transpose(1, 0, 2).reshape(n_all, 8 * share)
    parts = jnp.concatenate([parts, bias_up_whole.reshape(n_all, -1)], axis=1)
    parts = lax.all_to_all(parts, ALL, split_axis=0, concat_axis=0, tiled=True)
    own = jnp.sum(parts, axis=0)
    vec = own[: 8 * share].reshape(8, share)

    return (
        outputs,
        grad_inputs.reshape(seqs, span, width),
        grad_w_qkv,
        vec[0],
        vec[1],
        grad_w_out,
        vec[2],
        vec[3],
        vec[4],
        grad_w_up,
        own[8 * share :],
        grad_w_down,
        vec[5],
        vec[6],
        vec[7],
    )


def solution(mesh):
    tokens, ids, matrix, vector = P("dp", LINE, None), P("dp", LINE), P(ALL, None), P(ALL)
    placed = (
        tokens,
        ids,
        vector,
        vector,
        matrix,
        vector,
        vector,
        matrix,
        vector,
        vector,
        vector,
        matrix,
        vector,
        matrix,
        vector,
        tokens,
    )
    given = (
        tokens,
        tokens,
        matrix,
        vector,
        vector,
        matrix,
        vector,
        vector,
        vector,
        matrix,
        vector,
        matrix,
        vector,
        vector,
        vector,
    )
    return jax.shard_map(on_device, mesh=mesh, in_specs=placed, out_specs=given, check_vma=False)
```

```python
import jax
import jax.numpy as jnp
from jax import lax
from jax.experimental import pallas as pl
from jax.experimental.pallas import tpu as pltpu
from jax.sharding import PartitionSpec as P

HEAD_DIM = 128
EPSILON = 1e-05
ALL = ("dp", "seq", "fsdp")
LINE = ("seq", "fsdp")
FAR = ((0, 2), (1, 3))
f32 = jnp.float32
bf16 = jnp.bfloat16


def dot(left, right, dims):
    return lax.dot_general(left, right, (dims, ((), ())), preferred_element_type=f32)


def norm_parts(values):
    average = jnp.mean(values, axis=-1, keepdims=True)
    centered = values - average
    variance = jnp.mean(centered * centered, axis=-1, keepdims=True)
    scale = lax.rsqrt(variance + EPSILON)
    return centered * scale, scale


def norm_back(grad, gain, normal, scale):
    scaled = grad * gain
    return scale * (
        scaled
        - jnp.mean(scaled, axis=-1, keepdims=True)
        - normal * jnp.mean(scaled * normal, axis=-1, keepdims=True)
    )


def gelu_both(hidden):
    root = (2.0 / jnp.pi) ** 0.5
    square = hidden * hidden
    tanh = jnp.tanh(root * (hidden + 0.044715 * hidden * square))
    half = 0.5 * (1.0 + tanh)
    slope = half + 0.5 * hidden * (1.0 - tanh * tanh) * root * (1.0 + 3 * 0.044715 * square)
    return hidden * half, slope


def swap(value, axis, mask):
    return lax.ppermute(value, axis, [(i, i ^ mask) for i in range(lax.axis_size(axis))])


def hop(value, pairs):
    return lax.ppermute(value, "seq", list(pairs))


def in_plane():
    return lax.axis_size("dp") == 4 and lax.axis_size("seq") == 4 and lax.axis_size("fsdp") == 2


def after(value, *earlier):
    return lax.optimization_barrier((value,) + earlier)[0]


def assemble(shape, parts, copies, scalars):
    def body(s_ref, *refs):
        out, sems = refs[len(parts)], refs[len(parts) + 1]
        flights = []
        for number, (part, source, target) in enumerate(copies):
            flight = pltpu.make_async_copy(refs[part].at[source], out.at[target(s_ref)], sems.at[number])
            flight.start()
            flights.append(flight)
        for flight in flights:
            flight.wait()

    size = 2 * shape[-1]
    for extent in shape[:-1]:
        size *= extent
    return call(
        body,
        in_specs=[pl.BlockSpec(memory_space=pltpu.SMEM)] + [pl.BlockSpec(memory_space=pl.ANY)] * len(parts),
        out_specs=pl.BlockSpec(memory_space=pltpu.VMEM),
        out_shape=jax.ShapeDtypeStruct(shape, bf16),
        scratch_shapes=[pltpu.SemaphoreType.DMA((len(copies),))],
        cost_estimate=cost(flops=0, bytes_accessed=2 * size, transcendentals=0),
    )(jnp.stack(scalars).astype(jnp.int32), *parts)


def pick(whole, at, axis=0):
    return lax.dynamic_index_in_dim(whole, at, axis, keepdims=False)


def unxor(value, axis, at):
    shape = value.shape
    bit = 1
    while bit < shape[axis]:
        pairs = value.reshape(shape[:axis] + (-1, 2, bit) + shape[axis + 1 :])
        other = jnp.flip(pairs, axis + 1).reshape(shape)
        value = jnp.where((at & bit) != 0, other, value)
        bit *= 2
    return value


def scatter_one(parts):
    half = parts[0].shape[0] // 2
    low = parts[3].astype(bf16)
    return swap(low[:half], "dp", 1), swap(low[half:], "dp", 2)


def scatter_mid(parts, got):
    half = parts[0].shape[0] // 2
    one, two = parts[1].astype(f32), parts[2].astype(f32)
    two = jnp.concatenate([two[:half] + got[0].astype(f32), two[half:]], axis=0).astype(bf16)
    one = jnp.concatenate([one[:half], one[half:] + got[1].astype(f32)], axis=0).astype(bf16)
    return one, two


def scatter_send(mid):
    return swap(mid[0], "dp", 1), swap(mid[1], "dp", 2)


def scatter_two(parts, got):
    return scatter_send(scatter_mid(parts, got))


def scatter_sum(parts, got):
    return parts[0].astype(f32) + got[0].astype(f32) + got[1].astype(f32)


class Plane:
    def __init__(self, share, feed, width):
        self.dp, self.seq, self.core = [lax.axis_index(axis) for axis in ALL]
        self.near, self.far = self.seq & 1, self.seq >> 1
        self.share, self.feed_width, self.width = share, feed, width
        self.block = feed // 32

    def begin(self, send, inputs, weights, dy):
        w_out, w_up, self.w_down = weights
        self.dy = dy
        share, rows = self.share, dy.shape[0]
        half = rows // 2
        halves = send.reshape(4, 2, share + 16, -1)
        got = swap(pick(halves, 1 - self.core, 1), "fsdp", 1)
        both = jnp.stack([pick(halves, self.core, 1), got], axis=1)
        dy_one, dy_two = swap(dy, "dp", 1), swap(dy, "dp", 2)
        whole = w_up.reshape(share, 4, 2, 2, 2 * self.block)
        split = lambda near: pick(whole, near, 3).transpose(1, 0, 2, 3).reshape(4, share, 4 * self.block)
        near = swap(split(1 - self.near), "seq", 1)
        out_line = lax.all_gather(w_out, "seq", axis=0, tiled=False)
        block = [pick(both, self.seq)] + [swap(pick(both, self.seq ^ k), "seq", k) for k in (1, 2, 3)]
        block = after(jnp.stack(block), dy_one, dy_two, near)
        line = lax.all_gather(after(inputs, block), LINE, axis=0, tiled=False)

        one, two = swap(block, "dp", 1), swap(block, "dp", 2)
        dy_top = swap(after(dy_two[:half], block), "dp", 1)
        dy_low = swap(after(dy_one[half:], block), "dp", 2)
        self.dy_first = jnp.concatenate([dy, dy_one, dy_two, dy_top, dy_low], axis=0)
        one, two, dy_top, dy_low = lax.optimization_barrier((one, two, dy_top, dy_low))

        top, low = swap(two[:2], "dp", 1), swap(one[2:], "dp", 2)
        columns = jnp.stack([split(self.near), near], axis=1)
        self.up_rows = jnp.stack(
            [pick(columns, self.dp)] + [swap(after(pick(columns, self.dp ^ k), one), "dp", k) for k in (1, 2, 3)]
        )
        copies = []
        for k in range(4):
            for z in range(4):
                for f in range(2):
                    part, at = (k, z) if k < 3 else (3 + z // 2, z % 2)
                    target = lambda s, k=k, z=z, f=f: (s[0] ^ k, s[1] ^ z, s[2] ^ f)
                    copies.append((part, (at, f, slice(0, share)), target))
        parts = [block, one, two, top, low]
        shape = (4, 4, 2, share, block.shape[3])
        qkv_own = assemble(shape, parts, copies, [self.dp, self.seq, self.core]).reshape(self.width, -1)
        self.out_mine = out_line
        self.out_one, self.out_two = [swap(after(out_line, self.up_rows, qkv_own), "dp", k) for k in (1, 2)]
        self.dy_near = swap(after(dy, self.up_rows, qkv_own), "seq", 1)
        line = after(line, self.out_one, self.out_two, self.dy_near)

        small = [block[:, :, share], one[:, :, share], two[:, :, share]]
        small.append(jnp.concatenate([top[:, :, share], low[:, :, share]], axis=0))
        small = unxor(unxor(unxor(jnp.stack(small), 0, self.dp), 1, self.seq), 2, self.core).reshape(32, -1)
        ids = unxor(unxor(block[:, :, share + 1, :rows], 0, self.seq), 1, self.core).reshape(8, rows)
        return line, qkv_own, small, ids

    def tokens_there(self, tokens):
        self.down_line = lax.all_gather(
            after(self.w_down, tokens), "seq", axis=0, tiled=False, axis_index_groups=FAR
        )

    def before_scores(self, qkv):
        top = swap(after(self.out_two[:2], qkv), "dp", 1)
        low = swap(after(self.out_one[2:], qkv), "dp", 2)
        self.out_mine = [self.out_mine, self.out_one, self.out_two, jnp.concatenate([top, low], axis=0)]
        self.dy_one, self.dy_two = [swap(after(self.dy_near, qkv), "dp", k) for k in (1, 2)]
        return after(qkv, self.down_line, top, low, self.dy_one, self.dy_two)

    def out_start(self, context):
        self.out_mine = after(jnp.stack(self.out_mine), context)
        half = self.dy.shape[0] // 2
        self.dy_top = swap(after(self.dy_two[:half], context), "dp", 1)
        self.dy_low = swap(after(self.dy_one[half:], context), "dp", 2)
        return context

    def out(self, context):
        mine = self.out_mine
        other = swap(mine, "fsdp", 1)
        up = lax.all_gather(after(self.up_rows, context), "seq", axis=0, tiled=False, axis_index_groups=FAR)
        self.gathered = (up, self.down_line)
        context = after(context, self.dy_top, self.dy_low)
        copies = [
            (f, (k, z), lambda s, f=f, k=k, z=z: (s[0] ^ k, z, s[1] ^ f))
            for f in range(2)
            for k in range(4)
            for z in range(4)
        ]
        whole = assemble(
            (4, 4, 2, self.share, self.width), [mine, other], copies, [self.dp, self.core]
        )
        return whole.reshape(self.width, self.width), context

    def gather(self, normed):
        half = normed.shape[0] // 2
        parts = [self.dy_near, self.dy_one, self.dy_two, self.dy_top, self.dy_low]
        dy_second = jnp.concatenate(parts, axis=0)
        other = swap(normed, "seq", 1)
        one, two = swap(normed, "dp", 1), swap(normed, "dp", 2)
        halves = lax.optimization_barrier((two[:half], one[half:], other))
        top, low = swap(halves[0], "dp", 1), swap(halves[1], "dp", 2)
        up, down = [after(part, *halves) for part in self.gathered]
        up_other, down_other = swap(up, "fsdp", 1), swap(down, "fsdp", 1)
        first = jnp.concatenate([normed, one, two, top, low], axis=0)
        other_one, other_two = [swap(after(other, one, two), "dp", k) for k in (1, 2)]
        other_top, other_low = swap(other_two[:half], "dp", 1), swap(other_one[half:], "dp", 2)
        second = jnp.concatenate([other, other_one, other_two, other_top, other_low], axis=0)
        copies = [(f, (far,), lambda s, far=far, f=f: (far, s[0] ^ f)) for far in range(2) for f in range(2)]
        shape = (2, 2, self.block, self.width)
        down = assemble(shape, [down, down_other], copies, [self.core]).reshape(4 * self.block, self.width)
        copies = [
            (f, (far, k, n), lambda s, far=far, f=f, k=k, n=n: (s[0] ^ k, far, s[1] ^ n, s[2] ^ f))
            for far in range(2)
            for f in range(2)
            for k in range(4)
            for n in range(2)
        ]
        shape = (4, 2, 2, 2, self.share, 4 * self.block)
        up = assemble(shape, [up, up_other], copies, [self.dp, self.near, self.core])
        return [first, second], [self.dy_first, dy_second], up.reshape(self.width, 4 * self.block), down

    def bias(self, table):
        return pick(pick(table.reshape(4, 2, 2, 2, -1), self.dp).transpose(1, 0, 2, 3), self.near).reshape(1, -1)

    def bias_spread(self, own):
        whole = jnp.zeros((4, 2, 2, 2, self.block), f32)
        own = own.reshape(1, 2, 1, 2, self.block)
        return lax.dynamic_update_slice(whole, own, (self.dp, 0, self.near, 0, 0)).reshape(-1)

    def feed(self, groups, dys, up, down, bias):
        own_act, own_gh, own_gn = feed_forward(groups[0], dys[0], up, down, bias)
        own_parts = jnp.split(own_gn, 4)
        own_one = scatter_one(own_parts)
        act, gh, gn = feed_forward(after(groups[1], *own_one), dys[1], up, down, bias)
        own_two = scatter_two(own_parts, own_one)
        parts = jnp.split(after(gn, *own_two), 4)
        one = scatter_one(parts)
        acts, ghs = jnp.concatenate([own_act, act], axis=0), jnp.concatenate([own_gh, gh], axis=0)
        grad_down = dot(acts, jnp.concatenate(dys, axis=0), ((0,), (0,))).astype(bf16)
        mid = scatter_mid(parts, [after(part, grad_down) for part in one])
        two = scatter_send(mid)
        grad_up = dot(jnp.concatenate(groups, axis=0), after(ghs, *mid), ((0,), (0,))).astype(bf16)
        fed = dot(after(acts, *mid), down, ((1,), (0,))).astype(bf16)
        fed, raw = lax.optimization_barrier((fed, grad_up))
        other = after(scatter_sum(parts, two).astype(bf16), fed, raw)
        whole = grad_down.reshape(2, 2, self.block, self.width)
        theirs = swap(pick(whole, 1 - self.core, 1), "fsdp", 1)
        grad_down = (pick(whole, self.core, 1).astype(f32) + theirs.astype(f32)).astype(bf16)
        whole = raw.reshape(4, 2, 2, 2, self.share, -1)
        theirs = swap(pick(whole, 1 - self.core, 3), "fsdp", 1)
        grad_up = (pick(whole, self.core, 3).astype(f32) + theirs.astype(f32)).astype(bf16)
        grad_up = grad_up.transpose(1, 0, 2, 3, 4)
        grad_down = grad_down.reshape(2 * self.block, self.width)
        owned = [
            lax.psum_scatter(grad, "seq", scatter_dimension=0, tiled=True, axis_index_groups=FAR)
            for grad in (grad_down, grad_up.reshape(self.width // 2, -1))
        ]
        self.grad_down = owned[0]
        self.up_rows = owned[1].reshape(4, 2, self.share, -1)
        grad = scatter_sum(own_parts, own_two) + swap(other, "seq", 1).astype(f32)
        self.fed = [fed.reshape(2, 4, -1, self.width)[:, k] for k in range(4)]
        self.fed_one = scatter_one([after(part, other) for part in self.fed])
        self.grad_up = grad_up
        return after(grad, grad_down), ghs

    def before_exchange(self, grad_context):
        return after(grad_context, self.grad_up, *self.fed_one)

    def before_attention(self, got, sent, grad_out_w):
        self.fed_two = scatter_two(self.fed, [after(part, sent) for part in self.fed_one])
        whole = grad_out_w.reshape(4, 4, 2, self.share, self.width)
        theirs = swap(pick(whole, 1 - self.core, 2), "fsdp", 1)
        whole = (pick(whole, self.core, 2).astype(f32) + theirs.astype(f32)).astype(bf16)
        self.out_parts = [pick(whole, self.dp ^ k) for k in range(4)]
        return after(got, whole)

    def before_norm(self, grad_qkv):
        own, other = scatter_sum(self.fed, self.fed_two)
        other = swap(other.astype(bf16), "seq", 1)
        self.feed_out = own + other.astype(f32)
        self.out_two = scatter_two(self.out_parts, scatter_one(self.out_parts))
        return after(grad_qkv, other, *self.out_two)

    def last(self, normed, grad_qkv):
        out_parts, out_two = self.out_parts, self.out_two
        grad = dot(normed, grad_qkv, ((0,), (0,))).astype(bf16)
        parts = [pick(grad.reshape(4, -1, grad.shape[1]), self.dp ^ k) for k in range(4)]
        two = scatter_two(parts, scatter_one(parts))
        line = scatter_sum(out_parts, out_two).reshape(2, 2, self.share, self.width)
        away = pick(line, 1 - self.far)
        away = away + hop(away.astype(bf16), ((0, 1), (3, 2))).astype(f32)
        self.line = pick(line, self.far)
        self.across = hop(away.astype(bf16), ((1, 2), (2, 1)))
        grad_up = self.up_back_end(after(self.up_rows, *two))
        return scatter_sum(parts, two), grad_up, self.grad_down

    def out_end(self, home):
        line = self.line + after(self.across, home).astype(f32)
        return pick(line, self.near) + swap(pick(line, 1 - self.near).astype(bf16), "seq", 1).astype(f32)

    def up_back_end(self, rows):
        parts = [pick(rows, self.dp)] + [swap(pick(rows, self.dp ^ k), "dp", k) for k in (1, 2, 3)]
        parts = jnp.stack(parts)
        pair = [pick(parts, self.near, 1), swap(pick(parts, 1 - self.near, 1), "seq", 1)]
        wide = 2 * self.block

        def body(s_ref, own_ref, other_ref, out_ref):
            for n, ref in enumerate((own_ref, other_ref)):
                for k in range(4):
                    for far in range(2):
                        at = ((s_ref[0] ^ k) * 4 + far * 2 + (s_ref[1] ^ n)) * wide
                        piece = ref[k, :, far * wide : (far + 1) * wide]
                        out_ref[:, pl.ds(pl.multiple_of(at, wide), wide)] = piece.astype(f32)

        return call(
            body,
            in_specs=[pl.BlockSpec(memory_space=pltpu.SMEM)] + [pl.BlockSpec(memory_space=pltpu.VMEM)] * 2,
            out_specs=pl.BlockSpec(memory_space=pltpu.VMEM),
            out_shape=jax.ShapeDtypeStruct((self.share, self.feed_width), f32),
            cost_estimate=cost(flops=0, bytes_accessed=6 * self.share * self.feed_width, transcendentals=0),
        )(jnp.stack([self.dp, self.near]).astype(jnp.int32), *pair)


class General:
    def __init__(self, share, feed, width):
        self.dp, self.n_dp, self.line = lax.axis_index("dp"), lax.axis_size("dp"), lax.axis_size(LINE)
        self.share, self.feed_width = share, feed

    def begin(self, send, inputs, weights, dy):
        self.w_out, self.w_up, self.w_down = weights
        self.dy = dy
        line = lax.all_gather(inputs, LINE, axis=0, tiled=False)
        got = lax.all_to_all(send, LINE, split_axis=0, concat_axis=0, tiled=True)
        whole = lax.all_gather(got, "dp", axis=0, tiled=True)
        share = self.share
        ids = got[:, share + 1, : dy.shape[0]]
        return line, whole[:, :share].reshape(-1, got.shape[2]), whole[:, share], ids

    def tokens_there(self, tokens):
        pass

    def before_scores(self, qkv):
        return qkv

    def out_start(self, context):
        return context

    def out(self, context):
        return lax.all_gather(self.w_out, ALL, axis=0, tiled=True), context

    def gather(self, normed):
        groups = [
            jnp.split(lax.all_gather(block, "dp", axis=0, tiled=True), self.groups()) for block in (normed, self.dy)
        ]
        sent = self.w_up.reshape(self.share, self.n_dp, -1).transpose(1, 0, 2)
        rows = lax.all_to_all(sent, "dp", split_axis=0, concat_axis=0, tiled=True)
        rows = lax.all_gather(rows, LINE, axis=0, tiled=False).transpose(1, 0, 2, 3)
        up = rows.reshape(-1, self.feed_width // self.n_dp)
        return groups[0], groups[1], up, lax.all_gather(self.w_down, LINE, axis=0, tiled=True)

    def bias(self, table):
        return pick(table.reshape(self.n_dp, 1, -1), self.dp)

    def bias_spread(self, own):
        whole = jnp.zeros((self.n_dp, own.shape[0]), f32)
        return lax.dynamic_update_slice_in_dim(whole, own[None], self.dp, 0).reshape(-1)

    def groups(self):
        return 2 if self.n_dp % 2 == 0 else 1

    def scatter(self, groups):
        whole = jnp.concatenate(groups, axis=0)
        return lax.psum_scatter(whole, "dp", scatter_dimension=0, tiled=True).astype(f32)

    def feed(self, groups, dys, up, down, bias):
        own = self.feed_width // self.n_dp
        done = [feed_forward(x, dy, up, down, bias) for x, dy in zip(groups, dys)]
        acts, ghs = [jnp.concatenate([part[k] for part in done], axis=0) for k in range(2)]
        grad_down = dot(acts, jnp.concatenate(dys, axis=0), ((0,), (0,))).astype(bf16)
        self.grad_down = lax.psum_scatter(grad_down, LINE, scatter_dimension=0, tiled=True).astype(f32)
        rows = dot(jnp.concatenate(groups, axis=0), ghs, ((0,), (0,))).astype(bf16)
        rows = rows.reshape(self.n_dp, self.line, self.share, own).transpose(1, 0, 2, 3).reshape(-1, own)
        rows = lax.psum_scatter(rows, LINE, scatter_dimension=0, tiled=True).reshape(self.n_dp, self.share, own)
        rows = lax.all_to_all(rows, "dp", split_axis=0, concat_axis=0, tiled=True)
        self.grad_up = rows.transpose(1, 0, 2).reshape(self.share, self.feed_width).astype(f32)
        self.feed_out = self.scatter([dot(part[0], down, ((1,), (0,))).astype(bf16) for part in done])
        return self.scatter([part[2] for part in done]), ghs

    def before_exchange(self, grad_context):
        return grad_context

    def before_attention(self, got, sent, grad_out_w):
        self.grad_out = lax.psum_scatter(grad_out_w, ALL, scatter_dimension=0, tiled=True).astype(f32)
        return got

    def before_norm(self, grad_qkv):
        return grad_qkv

    def last(self, normed, grad_qkv):
        grad = dot(normed, grad_qkv, ((0,), (0,))).astype(bf16)
        grad = lax.psum_scatter(grad, "dp", scatter_dimension=0, tiled=True)
        return grad, self.grad_up, self.grad_down

    def out_end(self, home):
        return self.grad_out


BLOCK = 256
LOG2E = 1.4426950408889634
VMEM_BYTES = 56 * 2**20


COST = 1000


def cost(flops, bytes_accessed, transcendentals):
    return pl.CostEstimate(
        flops=flops // COST, bytes_accessed=bytes_accessed // COST, transcendentals=transcendentals // COST
    )


def call(body, **options):
    return pl.pallas_call(
        body, compiler_params=pltpu.CompilerParams(vmem_limit_bytes=VMEM_BYTES), **options
    )


def norm_project_body(x_ref, gain_ref, beta_ref, w_ref, bias_ref, normed_ref, out_ref):
    normal, _ = norm_parts(x_ref[...].astype(f32))
    normed = (normal * gain_ref[...] + beta_ref[...]).astype(bf16)
    normed_ref[...] = normed
    out_ref[...] = (dot(normed, w_ref[...], ((1,), (0,))) + bias_ref[...]).astype(bf16)


def norm_project(tokens, gain, beta, weight, bias):
    rows, width = tokens.shape
    out = weight.shape[1]
    tile = min(rows, 256)
    whole = lambda shape: pl.BlockSpec(shape, lambda i: (0, 0))
    part = lambda cols: pl.BlockSpec((tile, cols), lambda i: (i, 0))
    return call(
        norm_project_body,
        grid=(rows // tile,),
        in_specs=[part(width), whole((1, width)), whole((1, width)), whole(weight.shape), whole((1, out))],
        out_specs=[part(width), part(out)],
        out_shape=[jax.ShapeDtypeStruct((rows, width), bf16), jax.ShapeDtypeStruct((rows, out), bf16)],
        cost_estimate=cost(
            flops=2 * rows * width * out, bytes_accessed=4 * rows * width + 2 * out * (rows + width), transcendentals=0
        ),
    )(tokens, gain, beta, weight, bias)


def tile_scores(query, key, slope, first, ids_col, ids_row, score_scale):
    scores = dot(query, key, ((1,), (1,))) * (score_scale * LOG2E)
    shape = scores.shape
    apart = lax.broadcasted_iota(jnp.int32, shape, 0) + first - lax.broadcasted_iota(jnp.int32, shape, 1)
    scores = scores - slope * jnp.abs(apart).astype(f32)
    return jnp.where(ids_row <= ids_col, scores, -1e30)


def attend_body(score_scale, heads, slope_ref, idc_ref, idr_ref, qkv_ref, ctx_ref, lse_ref):
    blocks, _, span, _ = qkv_ref.shape
    length = blocks * span
    cols = heads * HEAD_DIM
    step = BLOCK // span

    def piece(low, high, at):
        return qkv_ref[low:high, 0, :, at : at + HEAD_DIM].reshape((high - low) * span, HEAD_DIM)

    for head in range(heads):
        at = head * HEAD_DIM
        for t in range(length // BLOCK):
            top = min(blocks, (t + 2) * step)
            rows = slice(t * BLOCK, (t + 1) * BLOCK)
            scores = tile_scores(
                piece(t * step, (t + 1) * step, at),
                piece(0, top, cols + at),
                slope_ref[0, head] * LOG2E,
                t * BLOCK,
                idc_ref[0, rows],
                idr_ref[0, :, : top * span],
                score_scale,
            )
            row_max = jnp.max(scores, axis=-1, keepdims=True)
            exponent = jnp.exp2(scores - row_max)
            total = jnp.sum(exponent, axis=-1, keepdims=True)
            probs = (exponent * (1.0 / total)).astype(bf16)
            context = dot(probs, piece(0, top, 2 * cols + at), ((1,), (0,)))
            ctx_ref[t * step : (t + 1) * step, 0, :, at : at + HEAD_DIM] = context.astype(bf16).reshape(
                step, span, HEAD_DIM
            )
            lse_ref[0, rows, head : head + 1] = row_max + jnp.log2(total)


def attend_back_body(score_scale, heads, slope_ref, idc_ref, idr_ref, qkv_ref, grad_ref, lse_ref, out_ref, gk_ref, gv_ref):
    blocks, _, span, _ = qkv_ref.shape
    length = blocks * span
    cols = heads * HEAD_DIM
    step = BLOCK // span

    def piece(ref, low, high, at):
        return ref[low:high, 0, :, at : at + HEAD_DIM].reshape((high - low) * span, HEAD_DIM)

    def put(low, high, at, value):
        out_ref[low:high, 0, :, at : at + HEAD_DIM] = value.astype(bf16).reshape(high - low, span, HEAD_DIM)

    for head in range(heads):
        at = head * HEAD_DIM
        gk_ref[...] = jnp.zeros_like(gk_ref)
        gv_ref[...] = jnp.zeros_like(gv_ref)
        for t in range(length // BLOCK):
            top = min(blocks, (t + 2) * step)
            rows = slice(t * BLOCK, (t + 1) * BLOCK)
            query = piece(qkv_ref, t * step, (t + 1) * step, at)
            key = piece(qkv_ref, 0, top, cols + at)
            grad = piece(grad_ref, t * step, (t + 1) * step, at)
            scores = tile_scores(
                query,
                key,
                slope_ref[0, head] * LOG2E,
                t * BLOCK,
                idc_ref[0, rows],
                idr_ref[0, :, : top * span],
                score_scale,
            )
            probs = jnp.exp2(scores - lse_ref[0, rows, head : head + 1])
            grad_probs = dot(grad, piece(qkv_ref, 0, top, 2 * cols + at), ((1,), (1,)))
            total = jnp.sum(probs * grad_probs, axis=-1, keepdims=True)
            grad_scores = (probs * (grad_probs - total) * score_scale).astype(bf16)
            put(t * step, (t + 1) * step, at, dot(grad_scores, key, ((1,), (0,))))
            gk_ref[: top * span] += dot(grad_scores, query, ((0,), (0,)))
            gv_ref[: top * span] += dot(probs.astype(bf16), grad, ((0,), (0,)))
        put(0, blocks, cols + at, gk_ref[...])
        put(0, blocks, 2 * cols + at, gv_ref[...])


def attention_specs(blocks, span, cols, length, heads):
    split = lambda width: pl.BlockSpec((blocks, 1, span, width), lambda s: (0, s, 0, 0))
    return (
        pl.BlockSpec(memory_space=pltpu.SMEM),
        pl.BlockSpec((1, length, 1), lambda s: (s, 0, 0)),
        pl.BlockSpec((1, 1, length), lambda s: (s, 0, 0)),
        split(3 * cols),
        split(cols),
        pl.BlockSpec((1, length, heads), lambda s: (s, 0, 0)),
    )


def attend(slopes, ids, qkv, score_scale):
    blocks, seqs, span, width = qkv.shape
    length, cols = blocks * span, width // 3
    heads = cols // HEAD_DIM
    smem, idc, idr, three, one, lse = attention_specs(blocks, span, cols, length, heads)
    return call(
        lambda *refs: attend_body(score_scale, heads, *refs),
        grid=(seqs,),
        in_specs=[smem, idc, idr, three],
        out_specs=[one, lse],
        out_shape=[
            jax.ShapeDtypeStruct((blocks, seqs, span, cols), bf16),
            jax.ShapeDtypeStruct((seqs, length, heads), f32),
        ],
        cost_estimate=cost(
            flops=4 * seqs * cols * length * length,
            bytes_accessed=8 * seqs * length * cols,
            transcendentals=seqs * heads * length * length,
        ),
    )(slopes, ids[:, :, None], ids[:, None, :], qkv)


def attend_back(slopes, ids, qkv, grad, stats, score_scale):
    blocks, seqs, span, width = qkv.shape
    length, cols = blocks * span, width // 3
    heads = cols // HEAD_DIM
    smem, idc, idr, three, one, lse = attention_specs(blocks, span, cols, length, heads)
    return call(
        lambda *refs: attend_back_body(score_scale, heads, *refs),
        grid=(seqs,),
        in_specs=[smem, idc, idr, three, one, lse],
        out_specs=three,
        out_shape=jax.ShapeDtypeStruct(qkv.shape, bf16),
        scratch_shapes=[pltpu.VMEM((length, HEAD_DIM), f32)] * 2,
        cost_estimate=cost(
            flops=10 * seqs * cols * length * length,
            bytes_accessed=14 * seqs * length * cols,
            transcendentals=seqs * heads * length * length,
        ),
    )(slopes, ids[:, :, None], ids[:, None, :], qkv, grad, stats)


def norm_one_back_body(g_ref, w_ref, x_ref, out_ref, gain_ref, beta_ref):
    grad = dot(g_ref[...], w_ref[...], ((1,), (1,)))
    normal, _ = norm_parts(x_ref[...].astype(f32))
    out_ref[...] = grad.astype(bf16)

    @pl.when(pl.program_id(0) == 0)
    def _():
        gain_ref[...] = jnp.zeros_like(gain_ref)
        beta_ref[...] = jnp.zeros_like(beta_ref)

    gain_ref[...] += jnp.sum(grad * normal, axis=0, keepdims=True)
    beta_ref[...] += jnp.sum(grad, axis=0, keepdims=True)


def norm_one_back(grad_qkv, weight, tokens):
    rows, width = tokens.shape
    inner = weight.shape[1]
    tile = min(rows, 256)
    whole = lambda shape: pl.BlockSpec(shape, lambda i: (0, 0))
    part = lambda cols: pl.BlockSpec((tile, cols), lambda i: (i, 0))
    return call(
        norm_one_back_body,
        grid=(rows // tile,),
        in_specs=[part(inner), whole(weight.shape), part(width)],
        out_specs=[part(width), whole((1, width)), whole((1, width))],
        out_shape=[
            jax.ShapeDtypeStruct((rows, width), bf16),
            jax.ShapeDtypeStruct((1, width), f32),
            jax.ShapeDtypeStruct((1, width), f32),
        ],
        cost_estimate=cost(
            flops=2 * rows * width * inner, bytes_accessed=4 * rows * width + 2 * inner * (rows + width), transcendentals=0
        ),
    )(grad_qkv, weight, tokens)


def feed_body(x_ref, dy_ref, up_ref, down_ref, bias_ref, act_ref, gh_ref, gn_ref):
    up = up_ref[...]
    hidden = dot(x_ref[...], up, ((1,), (0,))) + bias_ref[...]
    grad = dot(dy_ref[...], down_ref[...], ((1,), (1,)))
    activated, slope = gelu_both(hidden)
    act_ref[...] = activated.astype(bf16)
    grad = (grad * slope).astype(bf16)
    gh_ref[...] = grad
    gn_ref[...] = dot(grad, up, ((1,), (1,))).astype(bf16)


def feed_forward(x, dy, up, down, bias):
    rows, width = x.shape
    feed = up.shape[1]
    tile = 256
    whole = lambda shape: pl.BlockSpec(shape, lambda i: (0, 0), pipeline_mode=pl.Buffered(1))
    part = lambda cols: pl.BlockSpec((tile, cols), lambda i: (i, 0))
    return call(
        feed_body,
        grid=(rows // tile,),
        in_specs=[part(width), part(width), whole(up.shape), whole(down.shape), whole(bias.shape)],
        out_specs=[part(feed), part(feed), part(width)],
        out_shape=[jax.ShapeDtypeStruct((rows, feed), bf16)] * 2 + [jax.ShapeDtypeStruct((rows, width), bf16)],
        cost_estimate=cost(
            flops=6 * rows * width * feed,
            bytes_accessed=6 * rows * width + 4 * feed * (rows + width),
            transcendentals=rows * feed,
        ),
    )(x, dy, up, down, bias)


def on_device(
    inputs,
    block_ids,
    gain_one,
    beta_one,
    w_qkv,
    bias_query,
    bias_value,
    w_out,
    bias_out,
    gain_two,
    beta_two,
    w_up,
    bias_up,
    w_down,
    bias_down,
    cotangent,
):
    seqs, span, width = inputs.shape
    rows = seqs * span
    n_dp = lax.axis_size("dp")
    n_line = lax.axis_size(LINE)
    length = span * n_line
    share = w_qkv.shape[0]
    feed = w_up.shape[1]
    cols = width // n_line
    heads = cols // HEAD_DIM
    score_scale = HEAD_DIM ** (-0.5)
    line_at = lax.axis_index(LINE)

    feeder = (Plane if in_plane() else General)(share, feed, width)

    vectors = jnp.stack([gain_one, beta_one, bias_query, bias_value, bias_out, gain_two, beta_two, bias_down])
    small = jnp.concatenate([vectors.reshape(-1), bias_up])
    extra = jnp.zeros((16, 3 * cols), bf16)
    extra = extra.at[0, : small.shape[0]].set(small)
    extra = extra.at[1, :rows].set(block_ids.astype(bf16).reshape(-1))
    qkv_send = w_qkv.reshape(share, 3, n_line, cols).transpose(2, 0, 1, 3).reshape(n_line, share, 3 * cols)
    extra = jnp.broadcast_to(extra[None], (n_line,) + extra.shape)
    qkv_send = jnp.concatenate([qkv_send, extra], axis=1)
    grad_out = cotangent.reshape(rows, width)
    tokens_line, qkv_own, small_all, ids = feeder.begin(qkv_send, inputs, (w_out, w_up, w_down), grad_out)
    ids = ids.astype(f32).reshape(n_line, seqs, span).transpose(1, 0, 2).reshape(seqs, length)
    small_all = small_all[:, : small.shape[0]].astype(f32)
    vectors = small_all[:, : 8 * share].reshape(-1, 8, share).transpose(1, 0, 2).reshape(8, width)
    gain1, beta1, biasq, biasv, biaso, gain2, beta2, biasd = [vectors[i][None] for i in range(8)]
    up_bias = feeder.bias(small_all[:, 8 * share :])
    biasq_own = lax.dynamic_slice_in_dim(biasq, line_at * cols, cols, 1)
    biasv_own = lax.dynamic_slice_in_dim(biasv, line_at * cols, cols, 1)

    tokens_line = tokens_line.reshape(n_line * rows, width)
    tokens_line, qkv_own, vectors = lax.optimization_barrier((tokens_line, qkv_own, vectors))
    feeder.tokens_there(tokens_line)
    bias_row = jnp.concatenate([biasq_own, jnp.zeros_like(biasq_own), biasv_own], axis=1)
    normed_one, qkv = norm_project(tokens_line, gain1, beta1, qkv_own, bias_row)
    qkv = qkv.reshape(n_line, seqs, span, 3 * cols)
    qkv = feeder.before_scores(qkv)
    numbers = (line_at * heads + jnp.arange(heads)).astype(f32)
    slopes = jnp.exp2(-8.0 * (numbers + 1.0) / (n_line * heads))[None]
    context_own, stats = attend(slopes, ids, qkv, score_scale)
    context_own = context_own.reshape(n_line, rows, cols)
    context_own = feeder.out_start(context_own)
    context = lax.all_to_all(context_own, LINE, split_axis=0, concat_axis=0, tiled=True)
    out_full, context = feeder.out(context)
    context = context.transpose(1, 0, 2).reshape(rows, width)

    tokens = inputs.astype(f32).reshape(rows, width)
    residual = tokens + dot(context, out_full, ((1,), (0,))) + biaso
    normal_two, scale_two = norm_parts(residual)
    normed_two = (normal_two * gain2 + beta2).astype(bf16)

    normed_groups, grad_out_groups, up_own, down_own = feeder.gather(normed_two)
    grad_normed_two, grad_hidden = feeder.feed(normed_groups, grad_out_groups, up_own, down_own, up_bias)
    grad_out_f = grad_out.astype(f32)
    grad_residual = grad_out_f + norm_back(grad_normed_two, gain2, normal_two, scale_two)

    grad_branch = grad_residual.astype(bf16)
    grad_context = dot(grad_branch, out_full, ((1,), (1,))).astype(bf16)
    grad_context = grad_context.reshape(rows, n_line, cols).transpose(1, 0, 2)
    grad_context = feeder.before_exchange(grad_context)
    sent = grad_context
    grad_branch = after(grad_branch, sent)
    grad_context = lax.all_to_all(grad_context, LINE, split_axis=0, concat_axis=0, tiled=True)
    grad_out_w = dot(context, grad_branch, ((0,), (0,))).astype(bf16)
    grad_context = feeder.before_attention(grad_context, sent, grad_out_w).reshape(n_line, seqs, span, cols)
    grad_qkv = attend_back(slopes, ids, qkv, grad_context, stats, score_scale).reshape(n_line * rows, 3 * cols)
    grad_qkv = feeder.before_norm(grad_qkv)
    grad_normed_part, gain1_part, beta1_part = norm_one_back(grad_qkv, qkv_own, tokens_line)
    gain1_part, beta1_part = gain1_part[0], beta1_part[0]
    grad_normed_one = lax.psum_scatter(
        grad_normed_part, LINE, scatter_dimension=0, tiled=True
    ).astype(f32)
    normal_one, scale_one = norm_parts(tokens)
    grad_inputs = grad_residual + norm_back(grad_normed_one, gain1, normal_one, scale_one)
    grad_qkv_w, grad_w_up, grad_w_down = feeder.last(normed_one, grad_qkv)
    grad_qkv_w = grad_qkv_w.astype(bf16)

    grad_normed_late, grad_residual_late, grad_hidden_late, grad_qkv_late, gain1_part, beta1_part, grad_w_down = (
        lax.optimization_barrier(
            (grad_normed_two, grad_residual, grad_hidden, grad_qkv, gain1_part, beta1_part, grad_w_down, grad_qkv_w)
        )[:7]
    )
    grad_w_down = grad_w_down.astype(f32)
    gain2_part = jnp.sum(grad_normed_late * normal_two, axis=0)
    beta2_part = jnp.sum(grad_normed_late, axis=0)
    biasd_part = jnp.sum(grad_out_f, axis=0)
    biaso_part = jnp.sum(grad_residual_late, axis=0)
    bias_up_part = jnp.sum(grad_hidden_late.astype(f32), axis=0)
    bias_qkv_part = jnp.sum(grad_qkv_late.astype(f32), axis=0)
    outputs = (residual + feeder.feed_out + biasd).astype(bf16).reshape(seqs, span, width)
    qkv_home = lax.all_to_all(
        grad_qkv_w.reshape(n_line, share, 3 * cols), LINE, split_axis=0, concat_axis=0, tiled=True
    )
    grad_w_out = feeder.out_end(qkv_home)
    grad_w_qkv = (
        qkv_home.reshape(n_line, share, 3, cols)
        .transpose(1, 2, 0, 3)
        .reshape(share, 3 * width)
        .astype(f32)
    )

    def spread(own, count, at):
        return lax.dynamic_update_slice_in_dim(jnp.zeros((count,) + own.shape, f32), own[None], at, 0)

    biasq_part = spread(bias_qkv_part[:cols], n_line, line_at).reshape(-1)
    biasv_part = spread(bias_qkv_part[2 * cols :], n_line, line_at).reshape(-1)
    bias_up_whole = feeder.bias_spread(bias_up_part)
    parts = jnp.stack(
        [biasq_part, biasv_part, biaso_part, gain1_part, beta1_part, biasd_part, gain2_part, beta2_part]
    )
    n_all = n_dp * n_line
    parts = parts.reshape(8, n_all, share).transpose(1, 0, 2).reshape(n_all, 8 * share)
    parts = jnp.concatenate([parts, bias_up_whole.reshape(n_all, -1)], axis=1)
    parts = lax.all_to_all(after(parts, qkv_home), ALL, split_axis=0, concat_axis=0, tiled=True)
    own = jnp.sum(parts, axis=0)
    vec = own[: 8 * share].reshape(8, share)

    return (
        outputs,
        grad_inputs.reshape(seqs, span, width),
        grad_w_qkv,
        vec[0],
        vec[1],
        grad_w_out,
        vec[2],
        vec[3],
        vec[4],
        grad_w_up,
        own[8 * share :],
        grad_w_down,
        vec[5],
        vec[6],
        vec[7],
    )


def solution(mesh):
    tokens, ids, matrix, vector = P("dp", LINE, None), P("dp", LINE), P(ALL, None), P(ALL)
    placed = (
        tokens,
        ids,
        vector,
        vector,
        matrix,
        vector,
        vector,
        matrix,
        vector,
        vector,
        vector,
        matrix,
        vector,
        matrix,
        vector,
        tokens,
    )
    given = (
        tokens,
        tokens,
        matrix,
        vector,
        vector,
        matrix,
        vector,
        vector,
        vector,
        matrix,
        vector,
        matrix,
        vector,
        vector,
        vector,
    )
    return jax.shard_map(on_device, mesh=mesh, in_specs=placed, out_specs=given, check_vma=False)
```

```python
import jax
import jax.numpy as jnp
from jax import lax
from jax.experimental import pallas as pl
from jax.experimental.pallas import tpu as pltpu
from jax.sharding import PartitionSpec as P

HEAD_DIM = 128
EPSILON = 1e-05
ALL = ("dp", "seq", "fsdp")
LINE = ("seq", "fsdp")
FAR = ((0, 2), (1, 3))
f32 = jnp.float32
bf16 = jnp.bfloat16


def dot(left, right, dims):
    return lax.dot_general(left, right, (dims, ((), ())), preferred_element_type=f32)


def norm_parts(values):
    average = jnp.mean(values, axis=-1, keepdims=True)
    centered = values - average
    variance = jnp.mean(centered * centered, axis=-1, keepdims=True)
    scale = lax.rsqrt(variance + EPSILON)
    return centered * scale, scale


def norm_back(grad, gain, normal, scale):
    scaled = grad * gain
    return scale * (
        scaled
        - jnp.mean(scaled, axis=-1, keepdims=True)
        - normal * jnp.mean(scaled * normal, axis=-1, keepdims=True)
    )


def gelu_both(hidden):
    root = (2.0 / jnp.pi) ** 0.5
    square = hidden * hidden
    tanh = jnp.tanh(root * (hidden + 0.044715 * hidden * square))
    half = 0.5 * (1.0 + tanh)
    slope = half + 0.5 * hidden * (1.0 - tanh * tanh) * root * (1.0 + 3 * 0.044715 * square)
    return hidden * half, slope


def swap(value, axis, mask):
    return lax.ppermute(value, axis, [(i, i ^ mask) for i in range(lax.axis_size(axis))])


def hop(value, pairs):
    return lax.ppermute(value, "seq", list(pairs))


def in_plane():
    return lax.axis_size("dp") == 4 and lax.axis_size("seq") == 4 and lax.axis_size("fsdp") == 2


def after(value, *earlier):
    return lax.optimization_barrier((value,) + earlier)[0]


def assemble(shape, parts, copies, scalars):
    def body(s_ref, *refs):
        out, sems = refs[len(parts)], refs[len(parts) + 1]
        flights = []
        for number, (part, source, target) in enumerate(copies):
            flight = pltpu.make_async_copy(refs[part].at[source], out.at[target(s_ref)], sems.at[number])
            flight.start()
            flights.append(flight)
        for flight in flights:
            flight.wait()

    size = 2 * shape[-1]
    for extent in shape[:-1]:
        size *= extent
    return call(
        body,
        in_specs=[pl.BlockSpec(memory_space=pltpu.SMEM)] + [pl.BlockSpec(memory_space=pl.ANY)] * len(parts),
        out_specs=pl.BlockSpec(memory_space=pltpu.VMEM),
        out_shape=jax.ShapeDtypeStruct(shape, bf16),
        scratch_shapes=[pltpu.SemaphoreType.DMA((len(copies),))],
        cost_estimate=cost(flops=0, bytes_accessed=2 * size, transcendentals=0),
    )(jnp.stack(scalars).astype(jnp.int32), *parts)


def pick(whole, at, axis=0):
    return lax.dynamic_index_in_dim(whole, at, axis, keepdims=False)


def unxor(value, axis, at):
    shape = value.shape
    bit = 1
    while bit < shape[axis]:
        pairs = value.reshape(shape[:axis] + (-1, 2, bit) + shape[axis + 1 :])
        other = jnp.flip(pairs, axis + 1).reshape(shape)
        value = jnp.where((at & bit) != 0, other, value)
        bit *= 2
    return value


def scatter_one(parts):
    half = parts[0].shape[0] // 2
    low = parts[3].astype(bf16)
    return swap(low[:half], "dp", 1), swap(low[half:], "dp", 2)


def scatter_mid(parts, got):
    half = parts[0].shape[0] // 2
    one, two = parts[1].astype(f32), parts[2].astype(f32)
    two = jnp.concatenate([two[:half] + got[0].astype(f32), two[half:]], axis=0).astype(bf16)
    one = jnp.concatenate([one[:half], one[half:] + got[1].astype(f32)], axis=0).astype(bf16)
    return one, two


def scatter_send(mid):
    return swap(mid[0], "dp", 1), swap(mid[1], "dp", 2)


def scatter_two(parts, got):
    return scatter_send(scatter_mid(parts, got))


def scatter_sum(parts, got):
    return parts[0].astype(f32) + got[0].astype(f32) + got[1].astype(f32)


class Plane:
    def __init__(self, share, feed, width):
        self.dp, self.seq, self.core = [lax.axis_index(axis) for axis in ALL]
        self.near, self.far = self.seq & 1, self.seq >> 1
        self.share, self.feed_width, self.width = share, feed, width
        self.block = feed // 32

    def begin(self, send, inputs, weights, dy):
        w_out, w_up, self.w_down = weights
        self.dy = dy
        share, rows = self.share, dy.shape[0]
        half = rows // 2
        halves = send.reshape(4, 2, share + 16, -1)
        got = swap(pick(halves, 1 - self.core, 1), "fsdp", 1)
        both = jnp.stack([pick(halves, self.core, 1), got], axis=1)
        dy_one, dy_two = swap(dy, "dp", 1), swap(dy, "dp", 2)
        whole = w_up.reshape(share, 4, 2, 2, 2 * self.block)
        split = lambda near: pick(whole, near, 3).transpose(1, 0, 2, 3).reshape(4, share, 4 * self.block)
        near = swap(split(1 - self.near), "seq", 1)
        out_line = lax.all_gather(w_out, "seq", axis=0, tiled=False)
        block = [pick(both, self.seq)] + [swap(pick(both, self.seq ^ k), "seq", k) for k in (1, 2, 3)]
        block = after(jnp.stack(block), dy_one, dy_two, near)
        line = lax.all_gather(after(inputs, block), LINE, axis=0, tiled=False)

        one, two = swap(block, "dp", 1), swap(block, "dp", 2)
        dy_top = swap(after(dy_two[:half], block), "dp", 1)
        dy_low = swap(after(dy_one[half:], block), "dp", 2)
        self.dy_first = jnp.concatenate([dy, dy_one, dy_two, dy_top, dy_low], axis=0)
        one, two, dy_top, dy_low = lax.optimization_barrier((one, two, dy_top, dy_low))

        top, low = swap(two[:2], "dp", 1), swap(one[2:], "dp", 2)
        columns = jnp.stack([split(self.near), near], axis=1)
        self.up_rows = jnp.stack(
            [pick(columns, self.dp)] + [swap(after(pick(columns, self.dp ^ k), one), "dp", k) for k in (1, 2, 3)]
        )
        copies = []
        for k in range(4):
            for z in range(4):
                for f in range(2):
                    part, at = (k, z) if k < 3 else (3 + z // 2, z % 2)
                    target = lambda s, k=k, z=z, f=f: (s[0] ^ k, s[1] ^ z, s[2] ^ f)
                    copies.append((part, (at, f, slice(0, share)), target))
        parts = [block, one, two, top, low]
        shape = (4, 4, 2, share, block.shape[3])
        qkv_own = assemble(shape, parts, copies, [self.dp, self.seq, self.core]).reshape(self.width, -1)
        self.out_mine = out_line
        self.out_one, self.out_two = [swap(after(out_line, self.up_rows, qkv_own), "dp", k) for k in (1, 2)]
        self.dy_near = swap(after(dy, self.up_rows, qkv_own), "seq", 1)
        line = after(line, self.out_one, self.out_two, self.dy_near)

        small = [block[:, :, share], one[:, :, share], two[:, :, share]]
        small.append(jnp.concatenate([top[:, :, share], low[:, :, share]], axis=0))
        small = unxor(unxor(unxor(jnp.stack(small), 0, self.dp), 1, self.seq), 2, self.core).reshape(32, -1)
        ids = unxor(unxor(block[:, :, share + 1, :rows], 0, self.seq), 1, self.core).reshape(8, rows)
        return line, qkv_own, small, ids

    def tokens_there(self, tokens):
        self.down_line = lax.all_gather(
            after(self.w_down, tokens), "seq", axis=0, tiled=False, axis_index_groups=FAR
        )

    def before_scores(self, qkv):
        top = swap(after(self.out_two[:2], qkv), "dp", 1)
        low = swap(after(self.out_one[2:], qkv), "dp", 2)
        self.out_mine = [self.out_mine, self.out_one, self.out_two, jnp.concatenate([top, low], axis=0)]
        self.dy_one, self.dy_two = [swap(after(self.dy_near, qkv), "dp", k) for k in (1, 2)]
        return after(qkv, self.down_line, top, low, self.dy_one, self.dy_two)

    def out_start(self, context):
        self.out_mine = after(jnp.stack(self.out_mine), context)
        half = self.dy.shape[0] // 2
        self.dy_top = swap(after(self.dy_two[:half], context), "dp", 1)
        self.dy_low = swap(after(self.dy_one[half:], context), "dp", 2)
        return context

    def out(self, context):
        mine = self.out_mine
        other = swap(mine, "fsdp", 1)
        up = lax.all_gather(after(self.up_rows, context), "seq", axis=0, tiled=False, axis_index_groups=FAR)
        self.gathered = (up, self.down_line)
        context = after(context, self.dy_top, self.dy_low)
        copies = [
            (f, (k, z), lambda s, f=f, k=k, z=z: (s[0] ^ k, z, s[1] ^ f))
            for f in range(2)
            for k in range(4)
            for z in range(4)
        ]
        whole = assemble(
            (4, 4, 2, self.share, self.width), [mine, other], copies, [self.dp, self.core]
        )
        return whole.reshape(self.width, self.width), context

    def gather(self, normed):
        half = normed.shape[0] // 2
        parts = [self.dy_near, self.dy_one, self.dy_two, self.dy_top, self.dy_low]
        dy_second = jnp.concatenate(parts, axis=0)
        other = swap(normed, "seq", 1)
        one, two = swap(normed, "dp", 1), swap(normed, "dp", 2)
        halves = lax.optimization_barrier((two[:half], one[half:]))
        top, low = swap(halves[0], "dp", 1), swap(halves[1], "dp", 2)
        up, down = [after(part, top, low, other) for part in self.gathered]
        up_other, down_other = swap(up, "fsdp", 1), swap(down, "fsdp", 1)
        first = jnp.concatenate([normed, one, two, top, low], axis=0)
        other_one, other_two = [swap(after(other, one, two), "dp", k) for k in (1, 2)]
        other_top, other_low = swap(other_two[:half], "dp", 1), swap(other_one[half:], "dp", 2)
        second = jnp.concatenate([other, other_one, other_two, other_top, other_low], axis=0)
        copies = [(f, (far,), lambda s, far=far, f=f: (far, s[0] ^ f)) for far in range(2) for f in range(2)]
        shape = (2, 2, self.block, self.width)
        down = assemble(shape, [down, down_other], copies, [self.core]).reshape(4 * self.block, self.width)
        copies = [
            (f, (far, k, n), lambda s, far=far, f=f, k=k, n=n: (s[0] ^ k, far, s[1] ^ n, s[2] ^ f))
            for far in range(2)
            for f in range(2)
            for k in range(4)
            for n in range(2)
        ]
        shape = (4, 2, 2, 2, self.share, 4 * self.block)
        up = assemble(shape, [up, up_other], copies, [self.dp, self.near, self.core])
        return [first, second], [self.dy_first, dy_second], up.reshape(self.width, 4 * self.block), down

    def bias(self, table):
        return pick(pick(table.reshape(4, 2, 2, 2, -1), self.dp).transpose(1, 0, 2, 3), self.near).reshape(1, -1)

    def bias_spread(self, own):
        whole = jnp.zeros((4, 2, 2, 2, self.block), f32)
        own = own.reshape(1, 2, 1, 2, self.block)
        return lax.dynamic_update_slice(whole, own, (self.dp, 0, self.near, 0, 0)).reshape(-1)

    def feed(self, groups, dys, up, down, bias):
        own_act, own_gh, own_gn = feed_forward(groups[0], dys[0], up, down, bias)
        own_parts = jnp.split(own_gn, 4)
        own_one = scatter_one(own_parts)
        act, gh, gn = feed_forward(after(groups[1], *own_one), dys[1], up, down, bias)
        own_two = scatter_two(own_parts, own_one)
        parts = jnp.split(after(gn, *own_two), 4)
        one = scatter_one(parts)
        acts, ghs = jnp.concatenate([own_act, act], axis=0), jnp.concatenate([own_gh, gh], axis=0)
        grad_down = dot(acts, jnp.concatenate(dys, axis=0), ((0,), (0,))).astype(bf16)
        mid = scatter_mid(parts, [after(part, grad_down) for part in one])
        two = scatter_send(mid)
        grad_up = dot(jnp.concatenate(groups, axis=0), after(ghs, *mid), ((0,), (0,))).astype(bf16)
        fed = dot(after(acts, *mid), down, ((1,), (0,))).astype(bf16)
        fed, raw = lax.optimization_barrier((fed, grad_up))
        other = after(scatter_sum(parts, two).astype(bf16), fed, raw)
        whole = grad_down.reshape(2, 2, self.block, self.width)
        theirs = swap(pick(whole, 1 - self.core, 1), "fsdp", 1)
        grad_down = (pick(whole, self.core, 1).astype(f32) + theirs.astype(f32)).astype(bf16)
        whole = raw.reshape(4, 2, 2, 2, self.share, -1)
        theirs = swap(pick(whole, 1 - self.core, 3), "fsdp", 1)
        grad_up = (pick(whole, self.core, 3).astype(f32) + theirs.astype(f32)).astype(bf16)
        grad_up = grad_up.transpose(1, 0, 2, 3, 4)
        grad_down = grad_down.reshape(2 * self.block, self.width)
        owned = [
            lax.psum_scatter(grad, "seq", scatter_dimension=0, tiled=True, axis_index_groups=FAR)
            for grad in (grad_down, grad_up.reshape(self.width // 2, -1))
        ]
        self.grad_down = owned[0]
        self.up_rows = owned[1].reshape(4, 2, self.share, -1)
        grad = scatter_sum(own_parts, own_two) + swap(other, "seq", 1).astype(f32)
        self.fed = [fed.reshape(2, 4, -1, self.width)[:, k] for k in range(4)]
        self.fed_one = scatter_one([after(part, other) for part in self.fed])
        self.grad_up = grad_up
        return after(grad, grad_down), ghs

    def before_exchange(self, grad_context):
        return after(grad_context, self.grad_up, *self.fed_one)

    def before_attention(self, got, sent, grad_out_w):
        self.fed_two = scatter_two(self.fed, [after(part, sent) for part in self.fed_one])
        whole = grad_out_w.reshape(4, 4, 2, self.share, self.width)
        theirs = swap(pick(whole, 1 - self.core, 2), "fsdp", 1)
        whole = (pick(whole, self.core, 2).astype(f32) + theirs.astype(f32)).astype(bf16)
        self.out_parts = [pick(whole, self.dp ^ k) for k in range(4)]
        return after(got, whole)

    def before_norm(self, grad_qkv):
        own, other = scatter_sum(self.fed, self.fed_two)
        other = swap(other.astype(bf16), "seq", 1)
        self.feed_out = own + other.astype(f32)
        self.out_two = scatter_two(self.out_parts, scatter_one(self.out_parts))
        return after(grad_qkv, other, *self.out_two)

    def last(self, normed, grad_qkv):
        out_parts, out_two = self.out_parts, self.out_two
        grad = dot(normed, grad_qkv, ((0,), (0,))).astype(bf16)
        parts = [pick(grad.reshape(4, -1, grad.shape[1]), self.dp ^ k) for k in range(4)]
        two = scatter_two(parts, scatter_one(parts))
        line = scatter_sum(out_parts, out_two).reshape(2, 2, self.share, self.width)
        away = pick(line, 1 - self.far)
        away = away + hop(away.astype(bf16), ((0, 1), (3, 2))).astype(f32)
        self.line = pick(line, self.far)
        self.across = hop(away.astype(bf16), ((1, 2), (2, 1)))
        grad_up = self.up_back_end(after(self.up_rows, *two))
        return scatter_sum(parts, two), grad_up, self.grad_down

    def out_end(self, home):
        line = self.line + after(self.across, home).astype(f32)
        return pick(line, self.near) + swap(pick(line, 1 - self.near).astype(bf16), "seq", 1).astype(f32)

    def up_back_end(self, rows):
        parts = [pick(rows, self.dp)] + [swap(pick(rows, self.dp ^ k), "dp", k) for k in (1, 2, 3)]
        parts = jnp.stack(parts)
        pair = [pick(parts, self.near, 1), swap(pick(parts, 1 - self.near, 1), "seq", 1)]
        wide = 2 * self.block

        def body(s_ref, own_ref, other_ref, out_ref):
            for n, ref in enumerate((own_ref, other_ref)):
                for k in range(4):
                    for far in range(2):
                        at = ((s_ref[0] ^ k) * 4 + far * 2 + (s_ref[1] ^ n)) * wide
                        piece = ref[k, :, far * wide : (far + 1) * wide]
                        out_ref[:, pl.ds(pl.multiple_of(at, wide), wide)] = piece.astype(f32)

        return call(
            body,
            in_specs=[pl.BlockSpec(memory_space=pltpu.SMEM)] + [pl.BlockSpec(memory_space=pltpu.VMEM)] * 2,
            out_specs=pl.BlockSpec(memory_space=pltpu.VMEM),
            out_shape=jax.ShapeDtypeStruct((self.share, self.feed_width), f32),
            cost_estimate=cost(flops=0, bytes_accessed=6 * self.share * self.feed_width, transcendentals=0),
        )(jnp.stack([self.dp, self.near]).astype(jnp.int32), *pair)


class General:
    def __init__(self, share, feed, width):
        self.dp, self.n_dp, self.line = lax.axis_index("dp"), lax.axis_size("dp"), lax.axis_size(LINE)
        self.share, self.feed_width = share, feed

    def begin(self, send, inputs, weights, dy):
        self.w_out, self.w_up, self.w_down = weights
        self.dy = dy
        line = lax.all_gather(inputs, LINE, axis=0, tiled=False)
        got = lax.all_to_all(send, LINE, split_axis=0, concat_axis=0, tiled=True)
        whole = lax.all_gather(got, "dp", axis=0, tiled=True)
        share = self.share
        ids = got[:, share + 1, : dy.shape[0]]
        return line, whole[:, :share].reshape(-1, got.shape[2]), whole[:, share], ids

    def tokens_there(self, tokens):
        pass

    def before_scores(self, qkv):
        return qkv

    def out_start(self, context):
        return context

    def out(self, context):
        return lax.all_gather(self.w_out, ALL, axis=0, tiled=True), context

    def gather(self, normed):
        groups = [
            jnp.split(lax.all_gather(block, "dp", axis=0, tiled=True), self.groups()) for block in (normed, self.dy)
        ]
        sent = self.w_up.reshape(self.share, self.n_dp, -1).transpose(1, 0, 2)
        rows = lax.all_to_all(sent, "dp", split_axis=0, concat_axis=0, tiled=True)
        rows = lax.all_gather(rows, LINE, axis=0, tiled=False).transpose(1, 0, 2, 3)
        up = rows.reshape(-1, self.feed_width // self.n_dp)
        return groups[0], groups[1], up, lax.all_gather(self.w_down, LINE, axis=0, tiled=True)

    def bias(self, table):
        return pick(table.reshape(self.n_dp, 1, -1), self.dp)

    def bias_spread(self, own):
        whole = jnp.zeros((self.n_dp, own.shape[0]), f32)
        return lax.dynamic_update_slice_in_dim(whole, own[None], self.dp, 0).reshape(-1)

    def groups(self):
        return 2 if self.n_dp % 2 == 0 else 1

    def scatter(self, groups):
        whole = jnp.concatenate(groups, axis=0)
        return lax.psum_scatter(whole, "dp", scatter_dimension=0, tiled=True).astype(f32)

    def feed(self, groups, dys, up, down, bias):
        own = self.feed_width // self.n_dp
        done = [feed_forward(x, dy, up, down, bias) for x, dy in zip(groups, dys)]
        acts, ghs = [jnp.concatenate([part[k] for part in done], axis=0) for k in range(2)]
        grad_down = dot(acts, jnp.concatenate(dys, axis=0), ((0,), (0,))).astype(bf16)
        self.grad_down = lax.psum_scatter(grad_down, LINE, scatter_dimension=0, tiled=True).astype(f32)
        rows = dot(jnp.concatenate(groups, axis=0), ghs, ((0,), (0,))).astype(bf16)
        rows = rows.reshape(self.n_dp, self.line, self.share, own).transpose(1, 0, 2, 3).reshape(-1, own)
        rows = lax.psum_scatter(rows, LINE, scatter_dimension=0, tiled=True).reshape(self.n_dp, self.share, own)
        rows = lax.all_to_all(rows, "dp", split_axis=0, concat_axis=0, tiled=True)
        self.grad_up = rows.transpose(1, 0, 2).reshape(self.share, self.feed_width).astype(f32)
        self.feed_out = self.scatter([dot(part[0], down, ((1,), (0,))).astype(bf16) for part in done])
        return self.scatter([part[2] for part in done]), ghs

    def before_exchange(self, grad_context):
        return grad_context

    def before_attention(self, got, sent, grad_out_w):
        self.grad_out = lax.psum_scatter(grad_out_w, ALL, scatter_dimension=0, tiled=True).astype(f32)
        return got

    def before_norm(self, grad_qkv):
        return grad_qkv

    def last(self, normed, grad_qkv):
        grad = dot(normed, grad_qkv, ((0,), (0,))).astype(bf16)
        grad = lax.psum_scatter(grad, "dp", scatter_dimension=0, tiled=True)
        return grad, self.grad_up, self.grad_down

    def out_end(self, home):
        return self.grad_out


BLOCK = 256
LOG2E = 1.4426950408889634
VMEM_BYTES = 56 * 2**20


COST = 1000


def cost(flops, bytes_accessed, transcendentals):
    return pl.CostEstimate(
        flops=flops // COST, bytes_accessed=bytes_accessed // COST, transcendentals=transcendentals // COST
    )


def call(body, **options):
    return pl.pallas_call(
        body, compiler_params=pltpu.CompilerParams(vmem_limit_bytes=VMEM_BYTES), **options
    )


def norm_project_body(x_ref, gain_ref, beta_ref, w_ref, bias_ref, normed_ref, out_ref):
    normal, _ = norm_parts(x_ref[...].astype(f32))
    normed = (normal * gain_ref[...] + beta_ref[...]).astype(bf16)
    normed_ref[...] = normed
    out_ref[...] = (dot(normed, w_ref[...], ((1,), (0,))) + bias_ref[...]).astype(bf16)


def norm_project(tokens, gain, beta, weight, bias):
    rows, width = tokens.shape
    out = weight.shape[1]
    tile = min(rows, 256)
    whole = lambda shape: pl.BlockSpec(shape, lambda i: (0, 0))
    part = lambda cols: pl.BlockSpec((tile, cols), lambda i: (i, 0))
    return call(
        norm_project_body,
        grid=(rows // tile,),
        in_specs=[part(width), whole((1, width)), whole((1, width)), whole(weight.shape), whole((1, out))],
        out_specs=[part(width), part(out)],
        out_shape=[jax.ShapeDtypeStruct((rows, width), bf16), jax.ShapeDtypeStruct((rows, out), bf16)],
        cost_estimate=cost(
            flops=2 * rows * width * out, bytes_accessed=4 * rows * width + 2 * out * (rows + width), transcendentals=0
        ),
    )(tokens, gain, beta, weight, bias)


def tile_scores(query, key, slope, first, ids_col, ids_row, score_scale):
    scores = dot(query, key, ((1,), (1,))) * (score_scale * LOG2E)
    shape = scores.shape
    apart = lax.broadcasted_iota(jnp.int32, shape, 0) + first - lax.broadcasted_iota(jnp.int32, shape, 1)
    scores = scores - slope * jnp.abs(apart).astype(f32)
    return jnp.where(ids_row <= ids_col, scores, -1e30)


def attend_body(score_scale, heads, slope_ref, idc_ref, idr_ref, qkv_ref, ctx_ref, lse_ref):
    blocks, _, span, _ = qkv_ref.shape
    length = blocks * span
    cols = heads * HEAD_DIM
    step = BLOCK // span

    def piece(low, high, at):
        return qkv_ref[low:high, 0, :, at : at + HEAD_DIM].reshape((high - low) * span, HEAD_DIM)

    for head in range(heads):
        at = head * HEAD_DIM
        for t in range(length // BLOCK):
            top = min(blocks, (t + 2) * step)
            rows = slice(t * BLOCK, (t + 1) * BLOCK)
            scores = tile_scores(
                piece(t * step, (t + 1) * step, at),
                piece(0, top, cols + at),
                slope_ref[0, head] * LOG2E,
                t * BLOCK,
                idc_ref[0, rows],
                idr_ref[0, :, : top * span],
                score_scale,
            )
            row_max = jnp.max(scores, axis=-1, keepdims=True)
            exponent = jnp.exp2(scores - row_max)
            total = jnp.sum(exponent, axis=-1, keepdims=True)
            probs = (exponent * (1.0 / total)).astype(bf16)
            context = dot(probs, piece(0, top, 2 * cols + at), ((1,), (0,)))
            ctx_ref[t * step : (t + 1) * step, 0, :, at : at + HEAD_DIM] = context.astype(bf16).reshape(
                step, span, HEAD_DIM
            )
            lse_ref[0, rows, head : head + 1] = row_max + jnp.log2(total)


def attend_back_body(score_scale, heads, slope_ref, idc_ref, idr_ref, qkv_ref, grad_ref, lse_ref, out_ref, gk_ref, gv_ref):
    blocks, _, span, _ = qkv_ref.shape
    length = blocks * span
    cols = heads * HEAD_DIM
    step = BLOCK // span

    def piece(ref, low, high, at):
        return ref[low:high, 0, :, at : at + HEAD_DIM].reshape((high - low) * span, HEAD_DIM)

    def put(low, high, at, value):
        out_ref[low:high, 0, :, at : at + HEAD_DIM] = value.astype(bf16).reshape(high - low, span, HEAD_DIM)

    for head in range(heads):
        at = head * HEAD_DIM
        gk_ref[...] = jnp.zeros_like(gk_ref)
        gv_ref[...] = jnp.zeros_like(gv_ref)
        for t in range(length // BLOCK):
            top = min(blocks, (t + 2) * step)
            rows = slice(t * BLOCK, (t + 1) * BLOCK)
            query = piece(qkv_ref, t * step, (t + 1) * step, at)
            key = piece(qkv_ref, 0, top, cols + at)
            grad = piece(grad_ref, t * step, (t + 1) * step, at)
            scores = tile_scores(
                query,
                key,
                slope_ref[0, head] * LOG2E,
                t * BLOCK,
                idc_ref[0, rows],
                idr_ref[0, :, : top * span],
                score_scale,
            )
            probs = jnp.exp2(scores - lse_ref[0, rows, head : head + 1])
            grad_probs = dot(grad, piece(qkv_ref, 0, top, 2 * cols + at), ((1,), (1,)))
            total = jnp.sum(probs * grad_probs, axis=-1, keepdims=True)
            grad_scores = (probs * (grad_probs - total) * score_scale).astype(bf16)
            put(t * step, (t + 1) * step, at, dot(grad_scores, key, ((1,), (0,))))
            gk_ref[: top * span] += dot(grad_scores, query, ((0,), (0,)))
            gv_ref[: top * span] += dot(probs.astype(bf16), grad, ((0,), (0,)))
        put(0, blocks, cols + at, gk_ref[...])
        put(0, blocks, 2 * cols + at, gv_ref[...])


def attention_specs(blocks, span, cols, length, heads):
    split = lambda width: pl.BlockSpec((blocks, 1, span, width), lambda s: (0, s, 0, 0))
    return (
        pl.BlockSpec(memory_space=pltpu.SMEM),
        pl.BlockSpec((1, length, 1), lambda s: (s, 0, 0)),
        pl.BlockSpec((1, 1, length), lambda s: (s, 0, 0)),
        split(3 * cols),
        split(cols),
        pl.BlockSpec((1, length, heads), lambda s: (s, 0, 0)),
    )


def attend(slopes, ids, qkv, score_scale):
    blocks, seqs, span, width = qkv.shape
    length, cols = blocks * span, width // 3
    heads = cols // HEAD_DIM
    smem, idc, idr, three, one, lse = attention_specs(blocks, span, cols, length, heads)
    return call(
        lambda *refs: attend_body(score_scale, heads, *refs),
        grid=(seqs,),
        in_specs=[smem, idc, idr, three],
        out_specs=[one, lse],
        out_shape=[
            jax.ShapeDtypeStruct((blocks, seqs, span, cols), bf16),
            jax.ShapeDtypeStruct((seqs, length, heads), f32),
        ],
        cost_estimate=cost(
            flops=4 * seqs * cols * length * length,
            bytes_accessed=8 * seqs * length * cols,
            transcendentals=seqs * heads * length * length,
        ),
    )(slopes, ids[:, :, None], ids[:, None, :], qkv)


def attend_back(slopes, ids, qkv, grad, stats, score_scale):
    blocks, seqs, span, width = qkv.shape
    length, cols = blocks * span, width // 3
    heads = cols // HEAD_DIM
    smem, idc, idr, three, one, lse = attention_specs(blocks, span, cols, length, heads)
    return call(
        lambda *refs: attend_back_body(score_scale, heads, *refs),
        grid=(seqs,),
        in_specs=[smem, idc, idr, three, one, lse],
        out_specs=three,
        out_shape=jax.ShapeDtypeStruct(qkv.shape, bf16),
        scratch_shapes=[pltpu.VMEM((length, HEAD_DIM), f32)] * 2,
        cost_estimate=cost(
            flops=10 * seqs * cols * length * length,
            bytes_accessed=14 * seqs * length * cols,
            transcendentals=seqs * heads * length * length,
        ),
    )(slopes, ids[:, :, None], ids[:, None, :], qkv, grad, stats)


def norm_one_back_body(g_ref, w_ref, x_ref, out_ref, gain_ref, beta_ref):
    grad = dot(g_ref[...], w_ref[...], ((1,), (1,)))
    normal, _ = norm_parts(x_ref[...].astype(f32))
    out_ref[...] = grad.astype(bf16)

    @pl.when(pl.program_id(0) == 0)
    def _():
        gain_ref[...] = jnp.zeros_like(gain_ref)
        beta_ref[...] = jnp.zeros_like(beta_ref)

    gain_ref[...] += jnp.sum(grad * normal, axis=0, keepdims=True)
    beta_ref[...] += jnp.sum(grad, axis=0, keepdims=True)


def norm_one_back(grad_qkv, weight, tokens):
    rows, width = tokens.shape
    inner = weight.shape[1]
    tile = min(rows, 256)
    whole = lambda shape: pl.BlockSpec(shape, lambda i: (0, 0))
    part = lambda cols: pl.BlockSpec((tile, cols), lambda i: (i, 0))
    return call(
        norm_one_back_body,
        grid=(rows // tile,),
        in_specs=[part(inner), whole(weight.shape), part(width)],
        out_specs=[part(width), whole((1, width)), whole((1, width))],
        out_shape=[
            jax.ShapeDtypeStruct((rows, width), bf16),
            jax.ShapeDtypeStruct((1, width), f32),
            jax.ShapeDtypeStruct((1, width), f32),
        ],
        cost_estimate=cost(
            flops=2 * rows * width * inner, bytes_accessed=4 * rows * width + 2 * inner * (rows + width), transcendentals=0
        ),
    )(grad_qkv, weight, tokens)


def feed_body(x_ref, dy_ref, up_ref, down_ref, bias_ref, act_ref, gh_ref, gn_ref):
    up = up_ref[...]
    hidden = dot(x_ref[...], up, ((1,), (0,))) + bias_ref[...]
    grad = dot(dy_ref[...], down_ref[...], ((1,), (1,)))
    activated, slope = gelu_both(hidden)
    act_ref[...] = activated.astype(bf16)
    grad = (grad * slope).astype(bf16)
    gh_ref[...] = grad
    gn_ref[...] = dot(grad, up, ((1,), (1,))).astype(bf16)


def feed_forward(x, dy, up, down, bias):
    rows, width = x.shape
    feed = up.shape[1]
    tile = 256
    whole = lambda shape: pl.BlockSpec(shape, lambda i: (0, 0), pipeline_mode=pl.Buffered(1))
    part = lambda cols: pl.BlockSpec((tile, cols), lambda i: (i, 0))
    return call(
        feed_body,
        grid=(rows // tile,),
        in_specs=[part(width), part(width), whole(up.shape), whole(down.shape), whole(bias.shape)],
        out_specs=[part(feed), part(feed), part(width)],
        out_shape=[jax.ShapeDtypeStruct((rows, feed), bf16)] * 2 + [jax.ShapeDtypeStruct((rows, width), bf16)],
        cost_estimate=cost(
            flops=6 * rows * width * feed,
            bytes_accessed=6 * rows * width + 4 * feed * (rows + width),
            transcendentals=rows * feed,
        ),
    )(x, dy, up, down, bias)


def on_device(
    inputs,
    block_ids,
    gain_one,
    beta_one,
    w_qkv,
    bias_query,
    bias_value,
    w_out,
    bias_out,
    gain_two,
    beta_two,
    w_up,
    bias_up,
    w_down,
    bias_down,
    cotangent,
):
    seqs, span, width = inputs.shape
    rows = seqs * span
    n_dp = lax.axis_size("dp")
    n_line = lax.axis_size(LINE)
    length = span * n_line
    share = w_qkv.shape[0]
    feed = w_up.shape[1]
    cols = width // n_line
    heads = cols // HEAD_DIM
    score_scale = HEAD_DIM ** (-0.5)
    line_at = lax.axis_index(LINE)

    feeder = (Plane if in_plane() else General)(share, feed, width)

    vectors = jnp.stack([gain_one, beta_one, bias_query, bias_value, bias_out, gain_two, beta_two, bias_down])
    small = jnp.concatenate([vectors.reshape(-1), bias_up])
    extra = jnp.zeros((16, 3 * cols), bf16)
    extra = extra.at[0, : small.shape[0]].set(small)
    extra = extra.at[1, :rows].set(block_ids.astype(bf16).reshape(-1))
    qkv_send = w_qkv.reshape(share, 3, n_line, cols).transpose(2, 0, 1, 3).reshape(n_line, share, 3 * cols)
    extra = jnp.broadcast_to(extra[None], (n_line,) + extra.shape)
    qkv_send = jnp.concatenate([qkv_send, extra], axis=1)
    grad_out = cotangent.reshape(rows, width)
    tokens_line, qkv_own, small_all, ids = feeder.begin(qkv_send, inputs, (w_out, w_up, w_down), grad_out)
    ids = ids.astype(f32).reshape(n_line, seqs, span).transpose(1, 0, 2).reshape(seqs, length)
    small_all = small_all[:, : small.shape[0]].astype(f32)
    vectors = small_all[:, : 8 * share].reshape(-1, 8, share).transpose(1, 0, 2).reshape(8, width)
    gain1, beta1, biasq, biasv, biaso, gain2, beta2, biasd = [vectors[i][None] for i in range(8)]
    up_bias = feeder.bias(small_all[:, 8 * share :])
    biasq_own = lax.dynamic_slice_in_dim(biasq, line_at * cols, cols, 1)
    biasv_own = lax.dynamic_slice_in_dim(biasv, line_at * cols, cols, 1)

    tokens_line = tokens_line.reshape(n_line * rows, width)
    tokens_line, qkv_own, vectors = lax.optimization_barrier((tokens_line, qkv_own, vectors))
    feeder.tokens_there(tokens_line)
    bias_row = jnp.concatenate([biasq_own, jnp.zeros_like(biasq_own), biasv_own], axis=1)
    normed_one, qkv = norm_project(tokens_line, gain1, beta1, qkv_own, bias_row)
    qkv = qkv.reshape(n_line, seqs, span, 3 * cols)
    qkv = feeder.before_scores(qkv)
    numbers = (line_at * heads + jnp.arange(heads)).astype(f32)
    slopes = jnp.exp2(-8.0 * (numbers + 1.0) / (n_line * heads))[None]
    context_own, stats = attend(slopes, ids, qkv, score_scale)
    context_own = context_own.reshape(n_line, rows, cols)
    context_own = feeder.out_start(context_own)
    context = lax.all_to_all(context_own, LINE, split_axis=0, concat_axis=0, tiled=True)
    out_full, context = feeder.out(context)
    context = context.transpose(1, 0, 2).reshape(rows, width)

    tokens = inputs.astype(f32).reshape(rows, width)
    residual = tokens + dot(context, out_full, ((1,), (0,))) + biaso
    normal_two, scale_two = norm_parts(residual)
    normed_two = (normal_two * gain2 + beta2).astype(bf16)

    normed_groups, grad_out_groups, up_own, down_own = feeder.gather(normed_two)
    grad_normed_two, grad_hidden = feeder.feed(normed_groups, grad_out_groups, up_own, down_own, up_bias)
    grad_out_f = grad_out.astype(f32)
    grad_residual = grad_out_f + norm_back(grad_normed_two, gain2, normal_two, scale_two)

    grad_branch = grad_residual.astype(bf16)
    grad_context = dot(grad_branch, out_full, ((1,), (1,))).astype(bf16)
    grad_context = grad_context.reshape(rows, n_line, cols).transpose(1, 0, 2)
    grad_context = feeder.before_exchange(grad_context)
    sent = grad_context
    grad_branch = after(grad_branch, sent)
    grad_context = lax.all_to_all(grad_context, LINE, split_axis=0, concat_axis=0, tiled=True)
    grad_out_w = dot(context, grad_branch, ((0,), (0,))).astype(bf16)
    grad_context = feeder.before_attention(grad_context, sent, grad_out_w).reshape(n_line, seqs, span, cols)
    grad_qkv = attend_back(slopes, ids, qkv, grad_context, stats, score_scale).reshape(n_line * rows, 3 * cols)
    grad_qkv = feeder.before_norm(grad_qkv)
    grad_normed_part, gain1_part, beta1_part = norm_one_back(grad_qkv, qkv_own, tokens_line)
    gain1_part, beta1_part = gain1_part[0], beta1_part[0]
    grad_normed_one = lax.psum_scatter(
        grad_normed_part, LINE, scatter_dimension=0, tiled=True
    ).astype(f32)
    normal_one, scale_one = norm_parts(tokens)
    grad_inputs = grad_residual + norm_back(grad_normed_one, gain1, normal_one, scale_one)
    grad_qkv_w, grad_w_up, grad_w_down = feeder.last(normed_one, grad_qkv)
    grad_qkv_w = grad_qkv_w.astype(bf16)

    grad_normed_late, grad_residual_late, grad_hidden_late, grad_qkv_late, gain1_part, beta1_part, grad_w_down = (
        lax.optimization_barrier(
            (grad_normed_two, grad_residual, grad_hidden, grad_qkv, gain1_part, beta1_part, grad_w_down, grad_qkv_w)
        )[:7]
    )
    grad_w_down = grad_w_down.astype(f32)
    gain2_part = jnp.sum(grad_normed_late * normal_two, axis=0)
    beta2_part = jnp.sum(grad_normed_late, axis=0)
    biasd_part = jnp.sum(grad_out_f, axis=0)
    biaso_part = jnp.sum(grad_residual_late, axis=0)
    bias_up_part = jnp.sum(grad_hidden_late.astype(f32), axis=0)
    bias_qkv_part = jnp.sum(grad_qkv_late.astype(f32), axis=0)
    outputs = (residual + feeder.feed_out + biasd).astype(bf16).reshape(seqs, span, width)
    qkv_home = lax.all_to_all(
        grad_qkv_w.reshape(n_line, share, 3 * cols), LINE, split_axis=0, concat_axis=0, tiled=True
    )
    grad_w_out = feeder.out_end(qkv_home)
    grad_w_qkv = (
        qkv_home.reshape(n_line, share, 3, cols)
        .transpose(1, 2, 0, 3)
        .reshape(share, 3 * width)
        .astype(f32)
    )

    def spread(own, count, at):
        return lax.dynamic_update_slice_in_dim(jnp.zeros((count,) + own.shape, f32), own[None], at, 0)

    biasq_part = spread(bias_qkv_part[:cols], n_line, line_at).reshape(-1)
    biasv_part = spread(bias_qkv_part[2 * cols :], n_line, line_at).reshape(-1)
    bias_up_whole = feeder.bias_spread(bias_up_part)
    parts = jnp.stack(
        [biasq_part, biasv_part, biaso_part, gain1_part, beta1_part, biasd_part, gain2_part, beta2_part]
    )
    n_all = n_dp * n_line
    parts = parts.reshape(8, n_all, share).transpose(1, 0, 2).reshape(n_all, 8 * share)
    parts = jnp.concatenate([parts, bias_up_whole.reshape(n_all, -1)], axis=1)
    parts = lax.all_to_all(after(parts, qkv_home), ALL, split_axis=0, concat_axis=0, tiled=True)
    own = jnp.sum(parts, axis=0)
    vec = own[: 8 * share].reshape(8, share)

    return (
        outputs,
        grad_inputs.reshape(seqs, span, width),
        grad_w_qkv,
        vec[0],
        vec[1],
        grad_w_out,
        vec[2],
        vec[3],
        vec[4],
        grad_w_up,
        own[8 * share :],
        grad_w_down,
        vec[5],
        vec[6],
        vec[7],
    )


def solution(mesh):
    tokens, ids, matrix, vector = P("dp", LINE, None), P("dp", LINE), P(ALL, None), P(ALL)
    placed = (
        tokens,
        ids,
        vector,
        vector,
        matrix,
        vector,
        vector,
        matrix,
        vector,
        vector,
        vector,
        matrix,
        vector,
        matrix,
        vector,
        tokens,
    )
    given = (
        tokens,
        tokens,
        matrix,
        vector,
        vector,
        matrix,
        vector,
        vector,
        vector,
        matrix,
        vector,
        matrix,
        vector,
        vector,
        vector,
    )
    return jax.shard_map(on_device, mesh=mesh, in_specs=placed, out_specs=given, check_vma=False)
```

```python
import jax
import jax.numpy as jnp
from jax import lax
from jax.experimental import pallas as pl
from jax.experimental.pallas import tpu as pltpu
from jax.sharding import PartitionSpec as P

HEAD_DIM = 128
EPSILON = 1e-05
ALL = ("dp", "seq", "fsdp")
LINE = ("seq", "fsdp")
FAR = ((0, 2), (1, 3))
f32 = jnp.float32
bf16 = jnp.bfloat16


def dot(left, right, dims):
    return lax.dot_general(left, right, (dims, ((), ())), preferred_element_type=f32)


def norm_parts(values):
    average = jnp.mean(values, axis=-1, keepdims=True)
    centered = values - average
    variance = jnp.mean(centered * centered, axis=-1, keepdims=True)
    scale = lax.rsqrt(variance + EPSILON)
    return centered * scale, scale


def norm_back(grad, gain, normal, scale):
    scaled = grad * gain
    return scale * (
        scaled
        - jnp.mean(scaled, axis=-1, keepdims=True)
        - normal * jnp.mean(scaled * normal, axis=-1, keepdims=True)
    )


def gelu_both(hidden):
    root = (2.0 / jnp.pi) ** 0.5
    square = hidden * hidden
    tanh = jnp.tanh(root * (hidden + 0.044715 * hidden * square))
    half = 0.5 * (1.0 + tanh)
    slope = half + 0.5 * hidden * (1.0 - tanh * tanh) * root * (1.0 + 3 * 0.044715 * square)
    return hidden * half, slope


def swap(value, axis, mask):
    return lax.ppermute(value, axis, [(i, i ^ mask) for i in range(lax.axis_size(axis))])


def hop(value, pairs):
    return lax.ppermute(value, "seq", list(pairs))


def in_plane():
    return lax.axis_size("dp") == 4 and lax.axis_size("seq") == 4 and lax.axis_size("fsdp") == 2


def after(value, *earlier):
    return lax.optimization_barrier((value,) + earlier)[0]


def assemble(shape, parts, copies, scalars):
    def body(s_ref, *refs):
        out, sems = refs[len(parts)], refs[len(parts) + 1]
        flights = []
        for number, (part, source, target) in enumerate(copies):
            flight = pltpu.make_async_copy(refs[part].at[source], out.at[target(s_ref)], sems.at[number])
            flight.start()
            flights.append(flight)
        for flight in flights:
            flight.wait()

    size = 2 * shape[-1]
    for extent in shape[:-1]:
        size *= extent
    return call(
        body,
        in_specs=[pl.BlockSpec(memory_space=pltpu.SMEM)] + [pl.BlockSpec(memory_space=pl.ANY)] * len(parts),
        out_specs=pl.BlockSpec(memory_space=pltpu.VMEM),
        out_shape=jax.ShapeDtypeStruct(shape, bf16),
        scratch_shapes=[pltpu.SemaphoreType.DMA((len(copies),))],
        cost_estimate=cost(flops=0, bytes_accessed=2 * size, transcendentals=0),
    )(jnp.stack(scalars).astype(jnp.int32), *parts)


def pick(whole, at, axis=0):
    return lax.dynamic_index_in_dim(whole, at, axis, keepdims=False)


def unxor(value, axis, at):
    shape = value.shape
    bit = 1
    while bit < shape[axis]:
        pairs = value.reshape(shape[:axis] + (-1, 2, bit) + shape[axis + 1 :])
        other = jnp.flip(pairs, axis + 1).reshape(shape)
        value = jnp.where((at & bit) != 0, other, value)
        bit *= 2
    return value


def scatter_one(parts):
    half = parts[0].shape[0] // 2
    low = parts[3].astype(bf16)
    return swap(low[:half], "dp", 1), swap(low[half:], "dp", 2)


def scatter_mid(parts, got):
    half = parts[0].shape[0] // 2
    one, two = parts[1].astype(f32), parts[2].astype(f32)
    two = jnp.concatenate([two[:half] + got[0].astype(f32), two[half:]], axis=0).astype(bf16)
    one = jnp.concatenate([one[:half], one[half:] + got[1].astype(f32)], axis=0).astype(bf16)
    return one, two


def scatter_send(mid):
    return swap(mid[0], "dp", 1), swap(mid[1], "dp", 2)


def scatter_two(parts, got):
    return scatter_send(scatter_mid(parts, got))


def scatter_sum(parts, got):
    return parts[0].astype(f32) + got[0].astype(f32) + got[1].astype(f32)


class Plane:
    def __init__(self, share, feed, width):
        self.dp, self.seq, self.core = [lax.axis_index(axis) for axis in ALL]
        self.near, self.far = self.seq & 1, self.seq >> 1
        self.share, self.feed_width, self.width = share, feed, width
        self.block = feed // 32

    def begin(self, send, inputs, weights, dy):
        w_out, w_up, self.w_down = weights
        self.dy = dy
        share, rows = self.share, dy.shape[0]
        half = rows // 2
        halves = send.reshape(4, 2, share + 16, -1)
        got = swap(pick(halves, 1 - self.core, 1), "fsdp", 1)
        both = jnp.stack([pick(halves, self.core, 1), got], axis=1)
        dy_one, dy_two = swap(dy, "dp", 1), swap(dy, "dp", 2)
        whole = w_up.reshape(share, 4, 2, 2, 2 * self.block)
        split = lambda near: pick(whole, near, 3).transpose(1, 0, 2, 3).reshape(4, share, 4 * self.block)
        near = swap(split(1 - self.near), "seq", 1)
        out_line = lax.all_gather(w_out, "seq", axis=0, tiled=False)
        block = [pick(both, self.seq)] + [swap(pick(both, self.seq ^ k), "seq", k) for k in (1, 2, 3)]
        block = after(jnp.stack(block), dy_one, dy_two, near)
        line = lax.all_gather(after(inputs, block), LINE, axis=0, tiled=False)

        one, two = swap(block, "dp", 1), swap(block, "dp", 2)
        dy_top = swap(after(dy_two[:half], block), "dp", 1)
        dy_low = swap(after(dy_one[half:], block), "dp", 2)
        self.dy_first = jnp.concatenate([dy, dy_one, dy_two, dy_top, dy_low], axis=0)
        one, two, dy_top, dy_low = lax.optimization_barrier((one, two, dy_top, dy_low))

        top, low = swap(two[:2], "dp", 1), swap(one[2:], "dp", 2)
        columns = jnp.stack([split(self.near), near], axis=1)
        self.up_rows = jnp.stack(
            [pick(columns, self.dp)] + [swap(after(pick(columns, self.dp ^ k), one), "dp", k) for k in (1, 2, 3)]
        )
        copies = []
        for k in range(4):
            for z in range(4):
                for f in range(2):
                    part, at = (k, z) if k < 3 else (3 + z // 2, z % 2)
                    target = lambda s, k=k, z=z, f=f: (s[0] ^ k, s[1] ^ z, s[2] ^ f)
                    copies.append((part, (at, f, slice(0, share)), target))
        parts = [block, one, two, top, low]
        shape = (4, 4, 2, share, block.shape[3])
        qkv_own = assemble(shape, parts, copies, [self.dp, self.seq, self.core]).reshape(self.width, -1)
        self.out_mine = out_line
        self.out_one, self.out_two = [swap(after(out_line, self.up_rows, qkv_own), "dp", k) for k in (1, 2)]
        self.dy_near = swap(after(dy, self.up_rows, qkv_own), "seq", 1)
        line = after(line, self.out_one, self.out_two, self.dy_near)

        small = [block[:, :, share], one[:, :, share], two[:, :, share]]
        small.append(jnp.concatenate([top[:, :, share], low[:, :, share]], axis=0))
        small = unxor(unxor(unxor(jnp.stack(small), 0, self.dp), 1, self.seq), 2, self.core).reshape(32, -1)
        ids = unxor(unxor(block[:, :, share + 1, :rows], 0, self.seq), 1, self.core).reshape(8, rows)
        return line, qkv_own, small, ids

    def tokens_there(self, tokens):
        self.down_line = lax.all_gather(
            after(self.w_down, tokens), "seq", axis=0, tiled=False, axis_index_groups=FAR
        )

    def before_scores(self, qkv):
        top = swap(after(self.out_two[:2], qkv), "dp", 1)
        low = swap(after(self.out_one[2:], qkv), "dp", 2)
        self.out_mine = [self.out_mine, self.out_one, self.out_two, jnp.concatenate([top, low], axis=0)]
        self.dy_one, self.dy_two = [swap(after(self.dy_near, qkv), "dp", k) for k in (1, 2)]
        return after(qkv, self.down_line, top, low, self.dy_one, self.dy_two)

    def out_start(self, context):
        self.out_mine = after(jnp.stack(self.out_mine), context)
        half = self.dy.shape[0] // 2
        self.dy_top = swap(after(self.dy_two[:half], context), "dp", 1)
        self.dy_low = swap(after(self.dy_one[half:], context), "dp", 2)
        return context

    def out(self, context):
        mine = self.out_mine
        other = swap(mine, "fsdp", 1)
        up = lax.all_gather(after(self.up_rows, context), "seq", axis=0, tiled=False, axis_index_groups=FAR)
        self.gathered = (up, self.down_line)
        context = after(context, self.dy_top, self.dy_low)
        copies = [
            (f, (k, z), lambda s, f=f, k=k, z=z: (s[0] ^ k, z, s[1] ^ f))
            for f in range(2)
            for k in range(4)
            for z in range(4)
        ]
        whole = assemble(
            (4, 4, 2, self.share, self.width), [mine, other], copies, [self.dp, self.core]
        )
        return whole.reshape(self.width, self.width), context

    def gather(self, normed):
        half = normed.shape[0] // 2
        parts = [self.dy_near, self.dy_one, self.dy_two, self.dy_top, self.dy_low]
        dy_second = jnp.concatenate(parts, axis=0)
        other = swap(normed, "seq", 1)
        one, two = swap(normed, "dp", 1), swap(normed, "dp", 2)
        halves = lax.optimization_barrier((two[:half], one[half:]))
        top, low = swap(halves[0], "dp", 1), swap(halves[1], "dp", 2)
        up, down = [after(part, top, low, other) for part in self.gathered]
        up_other, down_other = swap(up, "fsdp", 1), swap(down, "fsdp", 1)
        first = jnp.concatenate([normed, one, two, top, low], axis=0)
        other_one, other_two = [swap(after(other, one, two), "dp", k) for k in (1, 2)]
        other_top, other_low = swap(other_two[:half], "dp", 1), swap(other_one[half:], "dp", 2)
        second = jnp.concatenate([other, other_one, other_two, other_top, other_low], axis=0)
        copies = [(f, (far,), lambda s, far=far, f=f: (far, s[0] ^ f)) for far in range(2) for f in range(2)]
        shape = (2, 2, self.block, self.width)
        down = assemble(shape, [down, down_other], copies, [self.core]).reshape(4 * self.block, self.width)
        copies = [
            (f, (far, k, n), lambda s, far=far, f=f, k=k, n=n: (s[0] ^ k, far, s[1] ^ n, s[2] ^ f))
            for far in range(2)
            for f in range(2)
            for k in range(4)
            for n in range(2)
        ]
        shape = (4, 2, 2, 2, self.share, 4 * self.block)
        up = assemble(shape, [up, up_other], copies, [self.dp, self.near, self.core])
        return [first, second], [self.dy_first, dy_second], up.reshape(self.width, 4 * self.block), down

    def bias(self, table):
        return pick(pick(table.reshape(4, 2, 2, 2, -1), self.dp).transpose(1, 0, 2, 3), self.near).reshape(1, -1)

    def bias_spread(self, own):
        whole = jnp.zeros((4, 2, 2, 2, self.block), f32)
        own = own.reshape(1, 2, 1, 2, self.block)
        return lax.dynamic_update_slice(whole, own, (self.dp, 0, self.near, 0, 0)).reshape(-1)

    def feed(self, groups, dys, up, down, bias):
        own_act, own_gh, own_gn = feed_forward(groups[0], dys[0], up, down, bias)
        own_parts = jnp.split(own_gn, 4)
        own_one = scatter_one(own_parts)
        act, gh, gn = feed_forward(after(groups[1], *own_one), dys[1], up, down, bias)
        own_two = scatter_two(own_parts, own_one)
        parts = jnp.split(after(gn, *own_two), 4)
        one = scatter_one(parts)
        acts, ghs = jnp.concatenate([own_act, act], axis=0), jnp.concatenate([own_gh, gh], axis=0)
        grad_down = dot(acts, jnp.concatenate(dys, axis=0), ((0,), (0,))).astype(bf16)
        mid = scatter_mid(parts, [after(part, grad_down) for part in one])
        two = scatter_send(mid)
        grad_up = dot(jnp.concatenate(groups, axis=0), after(ghs, *mid), ((0,), (0,))).astype(bf16)
        fed = dot(after(acts, *mid), down, ((1,), (0,))).astype(bf16)
        fed, raw = lax.optimization_barrier((fed, grad_up))
        other = after(scatter_sum(parts, two).astype(bf16), fed, raw)
        whole = grad_down.reshape(2, 2, self.block, self.width)
        theirs = swap(pick(whole, 1 - self.core, 1), "fsdp", 1)
        grad_down = (pick(whole, self.core, 1).astype(f32) + theirs.astype(f32)).astype(bf16)
        whole = raw.reshape(4, 2, 2, 2, self.share, -1)
        theirs = swap(pick(whole, 1 - self.core, 3), "fsdp", 1)
        grad_up = (pick(whole, self.core, 3).astype(f32) + theirs.astype(f32)).astype(bf16)
        grad_up = grad_up.transpose(1, 0, 2, 3, 4)
        grad_down = grad_down.reshape(2 * self.block, self.width)
        owned = [
            lax.psum_scatter(grad, "seq", scatter_dimension=0, tiled=True, axis_index_groups=FAR)
            for grad in (grad_down, grad_up.reshape(self.width // 2, -1))
        ]
        self.grad_down = owned[0]
        self.up_rows = owned[1].reshape(4, 2, self.share, -1)
        grad = scatter_sum(own_parts, own_two) + swap(other, "seq", 1).astype(f32)
        self.fed = [fed.reshape(2, 4, -1, self.width)[:, k] for k in range(4)]
        self.fed_one = scatter_one([after(part, other) for part in self.fed])
        self.grad_up = grad_up
        return after(grad, grad_down), ghs

    def before_exchange(self, grad_context):
        return after(grad_context, self.grad_up, *self.fed_one)

    def before_attention(self, got, sent, grad_out_w):
        self.fed_two = scatter_two(self.fed, [after(part, sent) for part in self.fed_one])
        whole = grad_out_w.reshape(4, 4, 2, self.share, self.width)
        theirs = swap(pick(whole, 1 - self.core, 2), "fsdp", 1)
        whole = (pick(whole, self.core, 2).astype(f32) + theirs.astype(f32)).astype(bf16)
        self.out_parts = [pick(whole, self.dp ^ k) for k in range(4)]
        return got

    def before_norm(self, grad_qkv):
        own, other = scatter_sum(self.fed, self.fed_two)
        other = swap(other.astype(bf16), "seq", 1)
        self.feed_out = own + other.astype(f32)
        self.out_two = scatter_two(self.out_parts, scatter_one(self.out_parts))
        return after(grad_qkv, other)

    def last(self, normed, grad_qkv):
        out_parts, out_two = self.out_parts, self.out_two
        grad = dot(normed, grad_qkv, ((0,), (0,))).astype(bf16)
        parts = [pick(grad.reshape(4, -1, grad.shape[1]), self.dp ^ k) for k in range(4)]
        two = scatter_two(parts, scatter_one(parts))
        line = scatter_sum(out_parts, out_two).reshape(2, 2, self.share, self.width)
        away = pick(line, 1 - self.far)
        away = away + hop(away.astype(bf16), ((0, 1), (3, 2))).astype(f32)
        self.line = pick(line, self.far)
        self.across = hop(away.astype(bf16), ((1, 2), (2, 1)))
        grad_up = self.up_back_end(after(self.up_rows, *two))
        return scatter_sum(parts, two), grad_up, self.grad_down

    def out_end(self, home):
        line = self.line + after(self.across, home).astype(f32)
        return pick(line, self.near) + swap(pick(line, 1 - self.near).astype(bf16), "seq", 1).astype(f32)

    def up_back_end(self, rows):
        parts = [pick(rows, self.dp)] + [swap(pick(rows, self.dp ^ k), "dp", k) for k in (1, 2, 3)]
        parts = jnp.stack(parts)
        pair = [pick(parts, self.near, 1), swap(pick(parts, 1 - self.near, 1), "seq", 1)]
        wide = 2 * self.block

        def body(s_ref, own_ref, other_ref, out_ref):
            for n, ref in enumerate((own_ref, other_ref)):
                for k in range(4):
                    for far in range(2):
                        at = ((s_ref[0] ^ k) * 4 + far * 2 + (s_ref[1] ^ n)) * wide
                        piece = ref[k, :, far * wide : (far + 1) * wide]
                        out_ref[:, pl.ds(pl.multiple_of(at, wide), wide)] = piece.astype(f32)

        return call(
            body,
            in_specs=[pl.BlockSpec(memory_space=pltpu.SMEM)] + [pl.BlockSpec(memory_space=pltpu.VMEM)] * 2,
            out_specs=pl.BlockSpec(memory_space=pltpu.VMEM),
            out_shape=jax.ShapeDtypeStruct((self.share, self.feed_width), f32),
            cost_estimate=cost(flops=0, bytes_accessed=6 * self.share * self.feed_width, transcendentals=0),
        )(jnp.stack([self.dp, self.near]).astype(jnp.int32), *pair)


class General:
    def __init__(self, share, feed, width):
        self.dp, self.n_dp, self.line = lax.axis_index("dp"), lax.axis_size("dp"), lax.axis_size(LINE)
        self.share, self.feed_width = share, feed

    def begin(self, send, inputs, weights, dy):
        self.w_out, self.w_up, self.w_down = weights
        self.dy = dy
        line = lax.all_gather(inputs, LINE, axis=0, tiled=False)
        got = lax.all_to_all(send, LINE, split_axis=0, concat_axis=0, tiled=True)
        whole = lax.all_gather(got, "dp", axis=0, tiled=True)
        share = self.share
        ids = got[:, share + 1, : dy.shape[0]]
        return line, whole[:, :share].reshape(-1, got.shape[2]), whole[:, share], ids

    def tokens_there(self, tokens):
        pass

    def before_scores(self, qkv):
        return qkv

    def out_start(self, context):
        return context

    def out(self, context):
        return lax.all_gather(self.w_out, ALL, axis=0, tiled=True), context

    def gather(self, normed):
        groups = [
            jnp.split(lax.all_gather(block, "dp", axis=0, tiled=True), self.groups()) for block in (normed, self.dy)
        ]
        sent = self.w_up.reshape(self.share, self.n_dp, -1).transpose(1, 0, 2)
        rows = lax.all_to_all(sent, "dp", split_axis=0, concat_axis=0, tiled=True)
        rows = lax.all_gather(rows, LINE, axis=0, tiled=False).transpose(1, 0, 2, 3)
        up = rows.reshape(-1, self.feed_width // self.n_dp)
        return groups[0], groups[1], up, lax.all_gather(self.w_down, LINE, axis=0, tiled=True)

    def bias(self, table):
        return pick(table.reshape(self.n_dp, 1, -1), self.dp)

    def bias_spread(self, own):
        whole = jnp.zeros((self.n_dp, own.shape[0]), f32)
        return lax.dynamic_update_slice_in_dim(whole, own[None], self.dp, 0).reshape(-1)

    def groups(self):
        return 2 if self.n_dp % 2 == 0 else 1

    def scatter(self, groups):
        whole = jnp.concatenate(groups, axis=0)
        return lax.psum_scatter(whole, "dp", scatter_dimension=0, tiled=True).astype(f32)

    def feed(self, groups, dys, up, down, bias):
        own = self.feed_width // self.n_dp
        done = [feed_forward(x, dy, up, down, bias) for x, dy in zip(groups, dys)]
        acts, ghs = [jnp.concatenate([part[k] for part in done], axis=0) for k in range(2)]
        grad_down = dot(acts, jnp.concatenate(dys, axis=0), ((0,), (0,))).astype(bf16)
        self.grad_down = lax.psum_scatter(grad_down, LINE, scatter_dimension=0, tiled=True).astype(f32)
        rows = dot(jnp.concatenate(groups, axis=0), ghs, ((0,), (0,))).astype(bf16)
        rows = rows.reshape(self.n_dp, self.line, self.share, own).transpose(1, 0, 2, 3).reshape(-1, own)
        rows = lax.psum_scatter(rows, LINE, scatter_dimension=0, tiled=True).reshape(self.n_dp, self.share, own)
        rows = lax.all_to_all(rows, "dp", split_axis=0, concat_axis=0, tiled=True)
        self.grad_up = rows.transpose(1, 0, 2).reshape(self.share, self.feed_width).astype(f32)
        self.feed_out = self.scatter([dot(part[0], down, ((1,), (0,))).astype(bf16) for part in done])
        return self.scatter([part[2] for part in done]), ghs

    def before_exchange(self, grad_context):
        return grad_context

    def before_attention(self, got, sent, grad_out_w):
        self.grad_out = lax.psum_scatter(grad_out_w, ALL, scatter_dimension=0, tiled=True).astype(f32)
        return got

    def before_norm(self, grad_qkv):
        return grad_qkv

    def last(self, normed, grad_qkv):
        grad = dot(normed, grad_qkv, ((0,), (0,))).astype(bf16)
        grad = lax.psum_scatter(grad, "dp", scatter_dimension=0, tiled=True)
        return grad, self.grad_up, self.grad_down

    def out_end(self, home):
        return self.grad_out


BLOCK = 256
LOG2E = 1.4426950408889634
VMEM_BYTES = 56 * 2**20


COST = 1000


def cost(flops, bytes_accessed, transcendentals):
    return pl.CostEstimate(
        flops=flops // COST, bytes_accessed=bytes_accessed // COST, transcendentals=transcendentals // COST
    )


def call(body, **options):
    return pl.pallas_call(
        body, compiler_params=pltpu.CompilerParams(vmem_limit_bytes=VMEM_BYTES), **options
    )


def norm_project_body(x_ref, gain_ref, beta_ref, w_ref, bias_ref, normed_ref, out_ref):
    normal, _ = norm_parts(x_ref[...].astype(f32))
    normed = (normal * gain_ref[...] + beta_ref[...]).astype(bf16)
    normed_ref[...] = normed
    out_ref[...] = (dot(normed, w_ref[...], ((1,), (0,))) + bias_ref[...]).astype(bf16)


def norm_project(tokens, gain, beta, weight, bias):
    rows, width = tokens.shape
    out = weight.shape[1]
    tile = min(rows, 256)
    whole = lambda shape: pl.BlockSpec(shape, lambda i: (0, 0))
    part = lambda cols: pl.BlockSpec((tile, cols), lambda i: (i, 0))
    return call(
        norm_project_body,
        grid=(rows // tile,),
        in_specs=[part(width), whole((1, width)), whole((1, width)), whole(weight.shape), whole((1, out))],
        out_specs=[part(width), part(out)],
        out_shape=[jax.ShapeDtypeStruct((rows, width), bf16), jax.ShapeDtypeStruct((rows, out), bf16)],
        cost_estimate=cost(
            flops=2 * rows * width * out, bytes_accessed=4 * rows * width + 2 * out * (rows + width), transcendentals=0
        ),
    )(tokens, gain, beta, weight, bias)


def tile_scores(query, key, slope, first, ids_col, ids_row, score_scale):
    scores = dot(query, key, ((1,), (1,))) * (score_scale * LOG2E)
    shape = scores.shape
    apart = lax.broadcasted_iota(jnp.int32, shape, 0) + first - lax.broadcasted_iota(jnp.int32, shape, 1)
    scores = scores - slope * jnp.abs(apart).astype(f32)
    return jnp.where(ids_row <= ids_col, scores, -1e30)


def attend_body(score_scale, heads, slope_ref, idc_ref, idr_ref, qkv_ref, ctx_ref, lse_ref):
    blocks, _, span, _ = qkv_ref.shape
    length = blocks * span
    cols = heads * HEAD_DIM
    step = BLOCK // span

    def piece(low, high, at):
        return qkv_ref[low:high, 0, :, at : at + HEAD_DIM].reshape((high - low) * span, HEAD_DIM)

    for head in range(heads):
        at = head * HEAD_DIM
        for t in range(length // BLOCK):
            top = min(blocks, (t + 2) * step)
            rows = slice(t * BLOCK, (t + 1) * BLOCK)
            scores = tile_scores(
                piece(t * step, (t + 1) * step, at),
                piece(0, top, cols + at),
                slope_ref[0, head] * LOG2E,
                t * BLOCK,
                idc_ref[0, rows],
                idr_ref[0, :, : top * span],
                score_scale,
            )
            row_max = jnp.max(scores, axis=-1, keepdims=True)
            exponent = jnp.exp2(scores - row_max)
            total = jnp.sum(exponent, axis=-1, keepdims=True)
            probs = (exponent * (1.0 / total)).astype(bf16)
            context = dot(probs, piece(0, top, 2 * cols + at), ((1,), (0,)))
            ctx_ref[t * step : (t + 1) * step, 0, :, at : at + HEAD_DIM] = context.astype(bf16).reshape(
                step, span, HEAD_DIM
            )
            lse_ref[0, rows, head : head + 1] = row_max + jnp.log2(total)


def attend_back_body(score_scale, heads, slope_ref, idc_ref, idr_ref, qkv_ref, grad_ref, lse_ref, out_ref, gk_ref, gv_ref):
    blocks, _, span, _ = qkv_ref.shape
    length = blocks * span
    cols = heads * HEAD_DIM
    step = BLOCK // span

    def piece(ref, low, high, at):
        return ref[low:high, 0, :, at : at + HEAD_DIM].reshape((high - low) * span, HEAD_DIM)

    def put(low, high, at, value):
        out_ref[low:high, 0, :, at : at + HEAD_DIM] = value.astype(bf16).reshape(high - low, span, HEAD_DIM)

    for head in range(heads):
        at = head * HEAD_DIM
        gk_ref[...] = jnp.zeros_like(gk_ref)
        gv_ref[...] = jnp.zeros_like(gv_ref)
        for t in range(length // BLOCK):
            top = min(blocks, (t + 2) * step)
            rows = slice(t * BLOCK, (t + 1) * BLOCK)
            query = piece(qkv_ref, t * step, (t + 1) * step, at)
            key = piece(qkv_ref, 0, top, cols + at)
            grad = piece(grad_ref, t * step, (t + 1) * step, at)
            scores = tile_scores(
                query,
                key,
                slope_ref[0, head] * LOG2E,
                t * BLOCK,
                idc_ref[0, rows],
                idr_ref[0, :, : top * span],
                score_scale,
            )
            probs = jnp.exp2(scores - lse_ref[0, rows, head : head + 1])
            grad_probs = dot(grad, piece(qkv_ref, 0, top, 2 * cols + at), ((1,), (1,)))
            total = jnp.sum(probs * grad_probs, axis=-1, keepdims=True)
            grad_scores = (probs * (grad_probs - total) * score_scale).astype(bf16)
            put(t * step, (t + 1) * step, at, dot(grad_scores, key, ((1,), (0,))))
            gk_ref[: top * span] += dot(grad_scores, query, ((0,), (0,)))
            gv_ref[: top * span] += dot(probs.astype(bf16), grad, ((0,), (0,)))
        put(0, blocks, cols + at, gk_ref[...])
        put(0, blocks, 2 * cols + at, gv_ref[...])


def attention_specs(blocks, span, cols, length, heads):
    split = lambda width: pl.BlockSpec((blocks, 1, span, width), lambda s: (0, s, 0, 0))
    return (
        pl.BlockSpec(memory_space=pltpu.SMEM),
        pl.BlockSpec((1, length, 1), lambda s: (s, 0, 0)),
        pl.BlockSpec((1, 1, length), lambda s: (s, 0, 0)),
        split(3 * cols),
        split(cols),
        pl.BlockSpec((1, length, heads), lambda s: (s, 0, 0)),
    )


def attend(slopes, ids, qkv, score_scale):
    blocks, seqs, span, width = qkv.shape
    length, cols = blocks * span, width // 3
    heads = cols // HEAD_DIM
    smem, idc, idr, three, one, lse = attention_specs(blocks, span, cols, length, heads)
    return call(
        lambda *refs: attend_body(score_scale, heads, *refs),
        grid=(seqs,),
        in_specs=[smem, idc, idr, three],
        out_specs=[one, lse],
        out_shape=[
            jax.ShapeDtypeStruct((blocks, seqs, span, cols), bf16),
            jax.ShapeDtypeStruct((seqs, length, heads), f32),
        ],
        cost_estimate=cost(
            flops=4 * seqs * cols * length * length,
            bytes_accessed=8 * seqs * length * cols,
            transcendentals=seqs * heads * length * length,
        ),
    )(slopes, ids[:, :, None], ids[:, None, :], qkv)


def attend_back(slopes, ids, qkv, grad, stats, score_scale):
    blocks, seqs, span, width = qkv.shape
    length, cols = blocks * span, width // 3
    heads = cols // HEAD_DIM
    smem, idc, idr, three, one, lse = attention_specs(blocks, span, cols, length, heads)
    return call(
        lambda *refs: attend_back_body(score_scale, heads, *refs),
        grid=(seqs,),
        in_specs=[smem, idc, idr, three, one, lse],
        out_specs=three,
        out_shape=jax.ShapeDtypeStruct(qkv.shape, bf16),
        scratch_shapes=[pltpu.VMEM((length, HEAD_DIM), f32)] * 2,
        cost_estimate=cost(
            flops=10 * seqs * cols * length * length,
            bytes_accessed=14 * seqs * length * cols,
            transcendentals=seqs * heads * length * length,
        ),
    )(slopes, ids[:, :, None], ids[:, None, :], qkv, grad, stats)


def norm_one_back_body(g_ref, w_ref, x_ref, out_ref, gain_ref, beta_ref):
    grad = dot(g_ref[...], w_ref[...], ((1,), (1,)))
    normal, _ = norm_parts(x_ref[...].astype(f32))
    out_ref[...] = grad.astype(bf16)

    @pl.when(pl.program_id(0) == 0)
    def _():
        gain_ref[...] = jnp.zeros_like(gain_ref)
        beta_ref[...] = jnp.zeros_like(beta_ref)

    gain_ref[...] += jnp.sum(grad * normal, axis=0, keepdims=True)
    beta_ref[...] += jnp.sum(grad, axis=0, keepdims=True)


def norm_one_back(grad_qkv, weight, tokens):
    rows, width = tokens.shape
    inner = weight.shape[1]
    tile = min(rows, 256)
    whole = lambda shape: pl.BlockSpec(shape, lambda i: (0, 0))
    part = lambda cols: pl.BlockSpec((tile, cols), lambda i: (i, 0))
    return call(
        norm_one_back_body,
        grid=(rows // tile,),
        in_specs=[part(inner), whole(weight.shape), part(width)],
        out_specs=[part(width), whole((1, width)), whole((1, width))],
        out_shape=[
            jax.ShapeDtypeStruct((rows, width), bf16),
            jax.ShapeDtypeStruct((1, width), f32),
            jax.ShapeDtypeStruct((1, width), f32),
        ],
        cost_estimate=cost(
            flops=2 * rows * width * inner, bytes_accessed=4 * rows * width + 2 * inner * (rows + width), transcendentals=0
        ),
    )(grad_qkv, weight, tokens)


def feed_body(x_ref, dy_ref, up_ref, down_ref, bias_ref, act_ref, gh_ref, gn_ref):
    up = up_ref[...]
    hidden = dot(x_ref[...], up, ((1,), (0,))) + bias_ref[...]
    grad = dot(dy_ref[...], down_ref[...], ((1,), (1,)))
    activated, slope = gelu_both(hidden)
    act_ref[...] = activated.astype(bf16)
    grad = (grad * slope).astype(bf16)
    gh_ref[...] = grad
    gn_ref[...] = dot(grad, up, ((1,), (1,))).astype(bf16)


def feed_forward(x, dy, up, down, bias):
    rows, width = x.shape
    feed = up.shape[1]
    tile = 256
    whole = lambda shape: pl.BlockSpec(shape, lambda i: (0, 0), pipeline_mode=pl.Buffered(1))
    part = lambda cols: pl.BlockSpec((tile, cols), lambda i: (i, 0))
    return call(
        feed_body,
        grid=(rows // tile,),
        in_specs=[part(width), part(width), whole(up.shape), whole(down.shape), whole(bias.shape)],
        out_specs=[part(feed), part(feed), part(width)],
        out_shape=[jax.ShapeDtypeStruct((rows, feed), bf16)] * 2 + [jax.ShapeDtypeStruct((rows, width), bf16)],
        cost_estimate=cost(
            flops=6 * rows * width * feed,
            bytes_accessed=6 * rows * width + 4 * feed * (rows + width),
            transcendentals=rows * feed,
        ),
    )(x, dy, up, down, bias)


def on_device(
    inputs,
    block_ids,
    gain_one,
    beta_one,
    w_qkv,
    bias_query,
    bias_value,
    w_out,
    bias_out,
    gain_two,
    beta_two,
    w_up,
    bias_up,
    w_down,
    bias_down,
    cotangent,
):
    seqs, span, width = inputs.shape
    rows = seqs * span
    n_dp = lax.axis_size("dp")
    n_line = lax.axis_size(LINE)
    length = span * n_line
    share = w_qkv.shape[0]
    feed = w_up.shape[1]
    cols = width // n_line
    heads = cols // HEAD_DIM
    score_scale = HEAD_DIM ** (-0.5)
    line_at = lax.axis_index(LINE)

    feeder = (Plane if in_plane() else General)(share, feed, width)

    vectors = jnp.stack([gain_one, beta_one, bias_query, bias_value, bias_out, gain_two, beta_two, bias_down])
    small = jnp.concatenate([vectors.reshape(-1), bias_up])
    extra = jnp.zeros((16, 3 * cols), bf16)
    extra = extra.at[0, : small.shape[0]].set(small)
    extra = extra.at[1, :rows].set(block_ids.astype(bf16).reshape(-1))
    qkv_send = w_qkv.reshape(share, 3, n_line, cols).transpose(2, 0, 1, 3).reshape(n_line, share, 3 * cols)
    extra = jnp.broadcast_to(extra[None], (n_line,) + extra.shape)
    qkv_send = jnp.concatenate([qkv_send, extra], axis=1)
    grad_out = cotangent.reshape(rows, width)
    tokens_line, qkv_own, small_all, ids = feeder.begin(qkv_send, inputs, (w_out, w_up, w_down), grad_out)
    ids = ids.astype(f32).reshape(n_line, seqs, span).transpose(1, 0, 2).reshape(seqs, length)
    small_all = small_all[:, : small.shape[0]].astype(f32)
    vectors = small_all[:, : 8 * share].reshape(-1, 8, share).transpose(1, 0, 2).reshape(8, width)
    gain1, beta1, biasq, biasv, biaso, gain2, beta2, biasd = [vectors[i][None] for i in range(8)]
    up_bias = feeder.bias(small_all[:, 8 * share :])
    biasq_own = lax.dynamic_slice_in_dim(biasq, line_at * cols, cols, 1)
    biasv_own = lax.dynamic_slice_in_dim(biasv, line_at * cols, cols, 1)

    tokens_line = tokens_line.reshape(n_line * rows, width)
    tokens_line, qkv_own, vectors = lax.optimization_barrier((tokens_line, qkv_own, vectors))
    feeder.tokens_there(tokens_line)
    bias_row = jnp.concatenate([biasq_own, jnp.zeros_like(biasq_own), biasv_own], axis=1)
    normed_one, qkv = norm_project(tokens_line, gain1, beta1, qkv_own, bias_row)
    qkv = qkv.reshape(n_line, seqs, span, 3 * cols)
    qkv = feeder.before_scores(qkv)
    numbers = (line_at * heads + jnp.arange(heads)).astype(f32)
    slopes = jnp.exp2(-8.0 * (numbers + 1.0) / (n_line * heads))[None]
    context_own, stats = attend(slopes, ids, qkv, score_scale)
    context_own = context_own.reshape(n_line, rows, cols)
    context_own = feeder.out_start(context_own)
    context = lax.all_to_all(context_own, LINE, split_axis=0, concat_axis=0, tiled=True)
    out_full, context = feeder.out(context)
    context = context.transpose(1, 0, 2).reshape(rows, width)

    tokens = inputs.astype(f32).reshape(rows, width)
    residual = tokens + dot(context, out_full, ((1,), (0,))) + biaso
    normal_two, scale_two = norm_parts(residual)
    normed_two = (normal_two * gain2 + beta2).astype(bf16)

    normed_groups, grad_out_groups, up_own, down_own = feeder.gather(normed_two)
    grad_normed_two, grad_hidden = feeder.feed(normed_groups, grad_out_groups, up_own, down_own, up_bias)
    grad_out_f = grad_out.astype(f32)
    grad_residual = grad_out_f + norm_back(grad_normed_two, gain2, normal_two, scale_two)

    grad_branch = grad_residual.astype(bf16)
    grad_context = dot(grad_branch, out_full, ((1,), (1,))).astype(bf16)
    grad_context = grad_context.reshape(rows, n_line, cols).transpose(1, 0, 2)
    grad_context = feeder.before_exchange(grad_context)
    sent = grad_context
    grad_branch = after(grad_branch, sent)
    grad_context = lax.all_to_all(grad_context, LINE, split_axis=0, concat_axis=0, tiled=True)
    grad_out_w = dot(context, grad_branch, ((0,), (0,))).astype(bf16)
    grad_context = feeder.before_attention(grad_context, sent, grad_out_w).reshape(n_line, seqs, span, cols)
    grad_qkv = attend_back(slopes, ids, qkv, grad_context, stats, score_scale).reshape(n_line * rows, 3 * cols)
    grad_qkv = feeder.before_norm(grad_qkv)
    grad_normed_part, gain1_part, beta1_part = norm_one_back(grad_qkv, qkv_own, tokens_line)
    gain1_part, beta1_part = gain1_part[0], beta1_part[0]
    grad_normed_one = lax.psum_scatter(
        grad_normed_part, LINE, scatter_dimension=0, tiled=True
    ).astype(f32)
    normal_one, scale_one = norm_parts(tokens)
    grad_inputs = grad_residual + norm_back(grad_normed_one, gain1, normal_one, scale_one)
    grad_qkv_w, grad_w_up, grad_w_down = feeder.last(normed_one, grad_qkv)
    grad_qkv_w = grad_qkv_w.astype(bf16)

    grad_normed_late, grad_residual_late, grad_hidden_late, grad_qkv_late, gain1_part, beta1_part, grad_w_down = (
        lax.optimization_barrier(
            (grad_normed_two, grad_residual, grad_hidden, grad_qkv, gain1_part, beta1_part, grad_w_down, grad_qkv_w)
        )[:7]
    )
    grad_w_down = grad_w_down.astype(f32)
    gain2_part = jnp.sum(grad_normed_late * normal_two, axis=0)
    beta2_part = jnp.sum(grad_normed_late, axis=0)
    biasd_part = jnp.sum(grad_out_f, axis=0)
    biaso_part = jnp.sum(grad_residual_late, axis=0)
    bias_up_part = jnp.sum(grad_hidden_late.astype(f32), axis=0)
    bias_qkv_part = jnp.sum(grad_qkv_late.astype(f32), axis=0)
    outputs = (residual + feeder.feed_out + biasd).astype(bf16).reshape(seqs, span, width)
    qkv_home = lax.all_to_all(
        grad_qkv_w.reshape(n_line, share, 3 * cols), LINE, split_axis=0, concat_axis=0, tiled=True
    )
    grad_w_out = feeder.out_end(qkv_home)
    grad_w_qkv = (
        qkv_home.reshape(n_line, share, 3, cols)
        .transpose(1, 2, 0, 3)
        .reshape(share, 3 * width)
        .astype(f32)
    )

    def spread(own, count, at):
        return lax.dynamic_update_slice_in_dim(jnp.zeros((count,) + own.shape, f32), own[None], at, 0)

    biasq_part = spread(bias_qkv_part[:cols], n_line, line_at).reshape(-1)
    biasv_part = spread(bias_qkv_part[2 * cols :], n_line, line_at).reshape(-1)
    bias_up_whole = feeder.bias_spread(bias_up_part)
    parts = jnp.stack(
        [biasq_part, biasv_part, biaso_part, gain1_part, beta1_part, biasd_part, gain2_part, beta2_part]
    )
    n_all = n_dp * n_line
    parts = parts.reshape(8, n_all, share).transpose(1, 0, 2).reshape(n_all, 8 * share)
    parts = jnp.concatenate([parts, bias_up_whole.reshape(n_all, -1)], axis=1)
    parts = lax.all_to_all(after(parts, qkv_home), ALL, split_axis=0, concat_axis=0, tiled=True)
    own = jnp.sum(parts, axis=0)
    vec = own[: 8 * share].reshape(8, share)

    return (
        outputs,
        grad_inputs.reshape(seqs, span, width),
        grad_w_qkv,
        vec[0],
        vec[1],
        grad_w_out,
        vec[2],
        vec[3],
        vec[4],
        grad_w_up,
        own[8 * share :],
        grad_w_down,
        vec[5],
        vec[6],
        vec[7],
    )


def solution(mesh):
    tokens, ids, matrix, vector = P("dp", LINE, None), P("dp", LINE), P(ALL, None), P(ALL)
    placed = (
        tokens,
        ids,
        vector,
        vector,
        matrix,
        vector,
        vector,
        matrix,
        vector,
        vector,
        vector,
        matrix,
        vector,
        matrix,
        vector,
        tokens,
    )
    given = (
        tokens,
        tokens,
        matrix,
        vector,
        vector,
        matrix,
        vector,
        vector,
        vector,
        matrix,
        vector,
        matrix,
        vector,
        vector,
        vector,
    )
    return jax.shard_map(on_device, mesh=mesh, in_specs=placed, out_specs=given, check_vma=False)
```
